32 devices in a mesh: seq: 8 (over y, x, core), chan: 4 (over z).
Axes of the slice: x: 2, y: 2, z: 4, core: 2. Of those that a mesh axis runs over, the one named last changes fastest.
Arguments:
- tokens: bfloat16 [4096, 8192], P('seq'), may hold values from -6 to 6
- proj_weight: bfloat16 [8192, 3, 2048], P('seq', None, 'chan'), may hold values from -0.0625 to 0.0625
- residues: float32 [16, 2048], P(None, 'chan'), may hold values from -1.5 to 1.5
- decay_rates: float32 [16, 2048], P(None, 'chan'), may hold values from 0.00012207031 to 0.05
- skip_gain: float32 [2048], P('chan'), may hold values from -3 to 3
- grad_out: bfloat16 [4096, 2048], P('seq', 'chan'), may hold values from -6 to 6
Outputs:
- gated_output: bfloat16 [4096, 2048], P('seq', 'chan')
- grad_tokens: bfloat16 [4096, 8192], P('seq', 'chan')
The draws below stay inside these ranges and needn't reach their ends.
All inputs are finite; a program needn't handle non-finite values.
Results may differ from the reference program's by a relative error of at most 0.022.
Values may be sent and summed in bfloat16 or wider, within the bound.
No kernel may reach another device: no remote copies, remote signals or barrier semaphores. Data moves between devices by JAX's collectives and lax.ppermute only.
A program may use at most 128 MiB of HBM per device.

```python
import jax
import jax.numpy as jnp
from jax import lax

D = 8192
C = 2048
MODES = 16
TOKENS = 4096
N_CHAN = 4


def draw_decay_rates(key, part):
    lowest = 0.5 / TOKENS
    highest = 0.05
    spread = jax.random.uniform(key, (MODES, C), jnp.float32)
    return lowest * jnp.exp(spread * jnp.log(highest / lowest))


def shard_levels(rng, dims, cuts, smallest, top_value):
    def one(axis_at, blocks):
        steps = jax.random.uniform(jax.random.fold_in(jax.random.fold_in(rng, 6), axis_at), (blocks,), jnp.float32, smallest / len(cuts), top_value / len(cuts))
        return jnp.repeat(jnp.exp(steps), dims[axis_at] // blocks).reshape((-1,) + (1,) * (len(dims) - axis_at - 1))

    level = one(*cuts[0])
    for cut in cuts[1:]:
        level = level * one(*cut)
    return level


def gaussian(rng, shape, deviation, most, pieces=(), kind=jnp.bfloat16):
    entries = deviation * jax.random.normal(rng, shape, jnp.float32)
    if pieces:
        entries = entries * shard_levels(rng, shape, pieces, -0.22, 0.18)
    return jnp.clip(entries, -most, most).astype(kind)


def setup_inputs(seed: int = 0) -> dict:
    keys = jax.random.split(jax.random.key(seed), 7)
    return {
        "tokens": gaussian(keys[0], (TOKENS, D), 1.0, 6.0, ((0, 8),)),
        "proj_weight": gaussian(keys[1], (D, 3, C), D ** -0.5, 0.0625, ((0, 8), (2, 4))),
        "residues": gaussian(keys[2], (MODES, C), 0.25, 1.5, ((1, 4),), jnp.float32),
        "decay_rates": draw_decay_rates(jax.random.fold_in(keys[6], 71), 0),
        "skip_gain": gaussian(keys[4], (C,), 0.5, 3.0, ((0, 4),), jnp.float32),
        "grad_out": gaussian(keys[5], (TOKENS, C), 1.0, 6.0, ((0, 8), (1, 4))),
    }


def modal_scan(signal, decay_step, mode_gain, backward):

    def advance(mode_state, token_row):
        mode_state = decay_step * mode_state + token_row[None, :]
        return (mode_state, lax.optimization_barrier(jnp.sum(mode_gain * mode_state, axis=0)))
    _, outputs = lax.scan(advance, jnp.zeros(decay_step.shape, jnp.float32), signal, reverse=backward)
    return outputs

def reference(tokens, proj_weight, residues, decay_rates, skip_gain, grad_out):
    flat_w = proj_weight.reshape(D, 3 * C)
    projected = jnp.dot(tokens, flat_w, preferred_element_type=jnp.float32)
    proj_vals = lax.optimization_barrier(projected.astype(jnp.bfloat16)).astype(jnp.float32).reshape(TOKENS, 3, C)
    query_in = proj_vals[:, 0]
    key_in = proj_vals[:, 1]
    value_in = proj_vals[:, 2]
    decay_step = jnp.exp(-decay_rates)
    mode_gain = residues * jnp.sqrt(-jnp.expm1(-2.0 * decay_rates))
    mixed_in = key_in * value_in
    filtered = modal_scan(mixed_in, decay_step, mode_gain, False) + skip_gain[None, :] * mixed_in
    gated_output = (query_in * filtered).astype(jnp.bfloat16)
    grad_gate = grad_out.astype(jnp.float32)
    grad_mix = grad_gate * query_in
    grad_query = grad_gate * filtered
    grad_conv = modal_scan(grad_mix, decay_step, mode_gain, True) + skip_gain[None, :] * grad_mix
    grad_proj = jnp.stack([grad_query, grad_conv * value_in, grad_conv * key_in], axis=1).astype(jnp.bfloat16)
    group_width = C // N_CHAN
    grouped = grad_proj.reshape(TOKENS, 3, N_CHAN, group_width)
    w_grouped = proj_weight.reshape(D, 3, N_CHAN, group_width)

    def add_group(group_id, running):
        grad_slab = lax.dynamic_index_in_dim(grouped, group_id, 2, keepdims=False).reshape(TOKENS, 3 * group_width)
        weight_slab = lax.dynamic_index_in_dim(w_grouped, group_id, 2, keepdims=False).reshape(D, 3 * group_width)
        slab_term = lax.dot_general(grad_slab, weight_slab, (((1,), (1,)), ((), ())), preferred_element_type=jnp.float32)
        return running + lax.optimization_barrier(slab_term.astype(jnp.bfloat16)).astype(jnp.float32)
    summed = lax.fori_loop(0, N_CHAN, add_group, jnp.zeros((TOKENS, D), jnp.float32))
    return (gated_output, summed.astype(jnp.bfloat16))
```

```python
import functools

import jax
import jax.numpy as jnp
from jax import lax
from jax.experimental import pallas as pl
from jax.experimental.pallas import tpu as pltpu
from jax.sharding import PartitionSpec as P

LANES = 128
SUBS = 8
MODES = 16
BLOCKS = 8
VMEM_BYTES = 48 * 1024 * 1024


def coefficients(residues, decay_rates, rows):
    return jnp.stack(
        [
            jnp.exp(-decay_rates),
            residues * jnp.sqrt(-jnp.expm1(-2.0 * decay_rates)),
            jnp.exp(-decay_rates * (rows // SUBS)),
            jnp.exp(-decay_rates * rows),
        ]
    )


def spread(coef_ref, which):
    table = coef_ref[which]
    return [jnp.broadcast_to(table[r : r + 1, :], (SUBS, LANES)) for r in range(MODES)]


def end_states(signal_ref, decay, run, backward):
    def step(j, state):
        at = run - 1 - j if backward else j
        row = signal_ref[pl.ds(at, SUBS, stride=run), :]
        return tuple(a * s + row for a, s in zip(decay, state))

    zero = jnp.zeros((SUBS, LANES), jnp.float32)
    return lax.fori_loop(0, run, step, (zero,) * MODES, unroll=8)


def full_scan(signal_ref, out_ref, decay, gain, state, run, backward):
    def step(j, state):
        at = run - 1 - j if backward else j
        rows = pl.ds(at, SUBS, stride=run)
        row = signal_ref[rows, :]
        state = tuple(a * s + row for a, s in zip(decay, state))
        terms = [g * s for g, s in zip(gain, state)]
        while len(terms) > 1:
            terms = [terms[i] + terms[i + 1] for i in range(0, len(terms), 2)]
        out_ref[rows, :] = terms[0]
        return state

    lax.fori_loop(0, run, step, tuple(state), unroll=8)


def project_kernel(run, order_ref, x_ref, w_ref, g_ref, coef_ref, proj_ref, runs_ref, ends_ref, acc, mix, gmix):
    k = pl.program_id(0)

    @pl.when(k == 0)
    def _():
        acc[...] = jnp.zeros_like(acc)

    x = x_ref[...]
    w = jnp.concatenate([w_ref[0, b] for b in range(3)], axis=1)
    acc[...] += jnp.dot(x, w, preferred_element_type=jnp.float32)

    @pl.when(k == pl.num_programs(0) - 1)
    def _():
        for b in range(3):
            proj_ref[b] = acc[:, b * LANES : (b + 1) * LANES].astype(jnp.bfloat16)
        mix[...] = proj_ref[1].astype(jnp.float32) * proj_ref[2].astype(jnp.float32)
        gmix[...] = g_ref[...].astype(jnp.float32) * proj_ref[0].astype(jnp.float32)
        decay = spread(coef_ref, 0)
        long = coef_ref[2]
        for way, signal in enumerate((mix, gmix)):
            state = end_states(signal, decay, run, way == 1)
            for r in range(MODES):
                runs_ref[way, pl.ds(r, SUBS, stride=MODES), :] = state[r]
            total = jnp.zeros((MODES, LANES), jnp.float32)
            for i in range(SUBS):
                at = SUBS - 1 - i if way else i
                total = long * total + runs_ref[way, at * MODES : (at + 1) * MODES, :]
            ends_ref[way] = total


def scan_kernel(run, place_ref, proj_ref, g_ref, coef_ref, skip_ref, runs_ref, ends_ref, gated_ref, gp_ref, mix, out, start):
    me = place_ref[0]
    count = ends_ref.shape[0]
    decay = spread(coef_ref, 0)
    gain = spread(coef_ref, 1)
    long = coef_ref[2]
    whole = coef_ref[3]
    skip = skip_ref[...]
    grad = g_ref[...].astype(jnp.float32)
    query = proj_ref[0].astype(jnp.float32)
    for way in range(2):
        state = jnp.zeros((MODES, LANES), jnp.float32)
        for i in range(count - 1):
            at = count - 1 - i if way else i
            keep = me < at if way else at < me
            state = jnp.where(keep, whole * state + ends_ref[at, way], state)
        for i in range(SUBS):
            at = SUBS - 1 - i if way else i
            start[at * MODES : (at + 1) * MODES, :] = state
            state = long * state + runs_ref[way, at * MODES : (at + 1) * MODES, :]
        first = [start[pl.ds(r, SUBS, stride=MODES), :] for r in range(MODES)]
        if way:
            mix[...] = grad * query
        else:
            mix[...] = proj_ref[1].astype(jnp.float32) * proj_ref[2].astype(jnp.float32)
        full_scan(mix, out, decay, gain, first, run, way == 1)
        filtered = out[...] + skip * mix[...]
        if way:
            gp_ref[:, LANES : 2 * LANES] = (filtered * proj_ref[2].astype(jnp.float32)).astype(jnp.bfloat16)
            gp_ref[:, 2 * LANES : 3 * LANES] = (filtered * proj_ref[1].astype(jnp.float32)).astype(jnp.bfloat16)
        else:
            gated_ref[...] = (query * filtered).astype(jnp.bfloat16)
            gp_ref[:, :LANES] = (grad * filtered).astype(jnp.bfloat16)


def project(order, tokens, pieces, grad_out, coef, chunk):
    rows, width = tokens.shape
    depth = width // BLOCKS
    run = rows // SUBS
    return pl.pallas_call(
        functools.partial(project_kernel, run),
        grid_spec=pltpu.PrefetchScalarGridSpec(
            num_scalar_prefetch=1,
            grid=(BLOCKS,),
            in_specs=[
                pl.BlockSpec((rows, depth), lambda k, order: (0, order[k])),
                pl.BlockSpec((1, 3, depth, LANES), lambda k, order: (k, 0, 0, 0)),
                pl.BlockSpec((rows, LANES), lambda k, order: (0, chunk)),
                pl.BlockSpec((4, MODES, LANES), lambda k, order: (0, 0, chunk)),
            ],
            out_specs=[
                pl.BlockSpec((3, rows, LANES), lambda k, order: (0, 0, 0)),
                pl.BlockSpec((2, SUBS * MODES, LANES), lambda k, order: (0, 0, 0)),
                pl.BlockSpec((2, MODES, LANES), lambda k, order: (0, 0, 0)),
            ],
            scratch_shapes=[
                pltpu.VMEM((rows, 3 * LANES), jnp.float32),
                pltpu.VMEM((rows, LANES), jnp.float32),
                pltpu.VMEM((rows, LANES), jnp.float32),
            ],
        ),
        out_shape=[
            jax.ShapeDtypeStruct((3, rows, LANES), jnp.bfloat16),
            jax.ShapeDtypeStruct((2, SUBS * MODES, LANES), jnp.float32),
            jax.ShapeDtypeStruct((2, MODES, LANES), jnp.float32),
        ],
        compiler_params=pltpu.CompilerParams(vmem_limit_bytes=VMEM_BYTES),
        cost_estimate=pl.CostEstimate(
            flops=2 * rows * width * 3 * LANES, bytes_accessed=2 * width * (rows + 3 * LANES), transcendentals=0
        ),
        name="project",
    )(order, tokens, pieces, grad_out, coef)


def scan(place, proj, grad_out, coef, skip, runs, ends, chunk):
    _, rows, _ = proj.shape
    run = rows // SUBS
    count = ends.shape[0]
    return pl.pallas_call(
        functools.partial(scan_kernel, run),
        grid_spec=pltpu.PrefetchScalarGridSpec(
            num_scalar_prefetch=1,
            grid=(1,),
            in_specs=[
                pl.BlockSpec((3, rows, LANES), lambda k, place: (0, 0, 0)),
                pl.BlockSpec((rows, LANES), lambda k, place: (0, chunk)),
                pl.BlockSpec((4, MODES, LANES), lambda k, place: (0, 0, chunk)),
                pl.BlockSpec((1, LANES), lambda k, place: (0, chunk)),
                pl.BlockSpec((2, SUBS * MODES, LANES), lambda k, place: (0, 0, 0)),
                pl.BlockSpec((count, 2, MODES, LANES), lambda k, place: (0, 0, 0, 0)),
            ],
            out_specs=[
                pl.BlockSpec((rows, LANES), lambda k, place: (0, 0)),
                pl.BlockSpec((rows, 3 * LANES), lambda k, place: (0, 0)),
            ],
            scratch_shapes=[
                pltpu.VMEM((rows, LANES), jnp.float32),
                pltpu.VMEM((rows, LANES), jnp.float32),
                pltpu.VMEM((SUBS * MODES, LANES), jnp.float32),
            ],
        ),
        out_shape=[
            jax.ShapeDtypeStruct((rows, LANES), jnp.bfloat16),
            jax.ShapeDtypeStruct((rows, 3 * LANES), jnp.bfloat16),
        ],
        compiler_params=pltpu.CompilerParams(vmem_limit_bytes=VMEM_BYTES),
        cost_estimate=pl.CostEstimate(flops=rows * LANES * MODES * 16, bytes_accessed=12 * rows * LANES, transcendentals=0),
        name="scan",
    )(place, proj, grad_out, coef, skip, runs, ends)


def input_grad_kernel(chunks, *refs):
    grads, weights, out_ref = refs[:chunks], refs[chunks : 2 * chunks], refs[-1]
    left = jnp.concatenate([g[...] for g in grads], axis=1)
    right = jnp.concatenate([w[0, b] for w in weights for b in range(3)], axis=1)
    total = lax.dot_general(left, right, (((1,), (1,)), ((), ())), preferred_element_type=jnp.float32)
    out_ref[...] = total.astype(out_ref.dtype)


def input_grad(grads, weights, first, stride, count):
    chunks = len(grads)
    rows = grads[0].shape[0]
    depth = weights[0].shape[2]
    return pl.pallas_call(
        functools.partial(input_grad_kernel, chunks),
        grid=(count,),
        in_specs=[pl.BlockSpec((rows, 3 * LANES), lambda i: (0, 0))] * chunks
        + [pl.BlockSpec((1, 3, depth, LANES), lambda i: (first + stride * i, 0, 0, 0))] * chunks,
        out_specs=pl.BlockSpec((rows, depth), lambda i: (0, i)),
        out_shape=jax.ShapeDtypeStruct((rows, count * depth), jnp.bfloat16),
        compiler_params=pltpu.CompilerParams(vmem_limit_bytes=VMEM_BYTES),
        cost_estimate=pl.CostEstimate(
            flops=2 * rows * count * depth * chunks * 3 * LANES,
            bytes_accessed=2 * count * depth * (rows + chunks * 3 * LANES),
            transcendentals=0,
        ),
        name="input_grad",
    )(*grads, *weights)


def gather_chunk(part):
    whole = lax.all_gather(part, "seq")
    count, _, depth, _ = whole.shape
    if count != BLOCKS:
        whole = whole.reshape(BLOCKS, count // BLOCKS, 3, depth, LANES).swapaxes(1, 2)
        whole = whole.reshape(BLOCKS, 3, count // BLOCKS * depth, LANES)
    return whole


def local(tokens, proj_weight, residues, decay_rates, skip_gain, grad_out):
    rows = tokens.shape[0]
    chunks = skip_gain.shape[0] // LANES
    place = lax.axis_index("seq").astype(jnp.int32).reshape(1)
    order = jnp.arange(BLOCKS, dtype=jnp.int32)
    coef = coefficients(residues, decay_rates, rows)
    skip = skip_gain[None, :]
    branches = proj_weight.swapaxes(0, 1)
    weights, gated, grads = [], [], []
    for c in range(chunks):
        whole = gather_chunk(branches[:, :, c * LANES : (c + 1) * LANES])
        weights.append(whole)
        proj, runs, ends = project(order, tokens, whole, grad_out, coef, c)
        ends = lax.all_gather(ends, "seq")
        gate, grad = scan(place, proj, grad_out, coef, skip, runs, ends, c)
        gated.append(gate)
        grads.append(grad)
    halves = []
    for h in range(2):
        dx = input_grad(grads, weights, h, 2, BLOCKS // 2)
        halves.append(lax.psum_scatter(dx, "chan", scatter_dimension=1, tiled=True))
    return (jnp.concatenate(gated, axis=1), jnp.concatenate(halves, axis=1))


def solution(mesh):
    placed = (
        P("seq", None),
        P("seq", None, "chan"),
        P(None, "chan"),
        P(None, "chan"),
        P("chan"),
        P("seq", "chan"),
    )
    return jax.shard_map(
        local,
        mesh=mesh,
        in_specs=placed,
        out_specs=(P("seq", "chan"), P("seq", "chan")),
        check_vma=False,
    )
```

```python
import functools

import jax
import jax.numpy as jnp
from jax import lax
from jax.experimental import pallas as pl
from jax.experimental.pallas import tpu as pltpu
from jax.sharding import PartitionSpec as P

LANES = 128
WIDTHS = (256, 128, 128)
SUBS = 8
MODES = 16
BLOCKS = 8
VMEM_BYTES = 60 * 1024 * 1024


def coefficients(residues, decay_rates, rows):
    return jnp.stack(
        [
            jnp.exp(-decay_rates),
            residues * jnp.sqrt(-jnp.expm1(-2.0 * decay_rates)),
            jnp.exp(-decay_rates * (rows // SUBS)),
            jnp.exp(-decay_rates * rows),
        ]
    )


def spread(coef_ref, which, lanes):
    table = coef_ref[which, :, lanes]
    return [jnp.broadcast_to(table[r : r + 1, :], (SUBS, LANES)) for r in range(MODES)]


def end_states(signal_ref, lanes, decay, run, backward):
    def step(j, state):
        at = run - 1 - j if backward else j
        row = signal_ref[pl.ds(at, SUBS, stride=run), lanes]
        return tuple(a * s + row for a, s in zip(decay, state))

    zero = jnp.zeros((SUBS, LANES), jnp.float32)
    return lax.fori_loop(0, run, step, (zero,) * MODES, unroll=8)


def full_scan(signal_ref, out_ref, decay, gain, state, run, backward):
    def step(j, state):
        at = run - 1 - j if backward else j
        rows = pl.ds(at, SUBS, stride=run)
        row = signal_ref[rows, :]
        state = tuple(a * s + row for a, s in zip(decay, state))
        terms = [g * s for g, s in zip(gain, state)]
        while len(terms) > 1:
            terms = [terms[i] + terms[i + 1] for i in range(0, len(terms), 2)]
        out_ref[rows, :] = terms[0]
        return state

    lax.fori_loop(0, run, step, tuple(state), unroll=8)


def branches_of(piece):
    return jnp.concatenate([piece[b] for b in range(3)], axis=1)


def bring(sources, targets, sems):
    copies = [pltpu.make_async_copy(a, b, sems.at[i]) for i, (a, b) in enumerate(zip(sources, targets))]
    for copy in copies:
        copy.start()
    return copies


def project_kernel(run, halves, order_ref, x_ref, *refs):
    count = sum(halves)
    pieces, (g_ref, coef_ref, proj_ref, runs_ref, ends_ref), refs = refs[:count], refs[count : count + 5], refs[count + 5 :]
    weights, (x, acc, mix, gmix, x_sems, w_sems) = refs[:count], refs[count:]
    width = g_ref.shape[1]
    depth = x_ref.shape[1] // len(halves)
    blocks = [x_ref.at[:, pl.ds(pl.multiple_of(order_ref[r] * depth, depth), depth)] for r in range(len(halves))]
    moves, parts_in = [], bring(pieces[:1], weights[:1], w_sems)
    moves = bring(blocks, [x.at[r] for r in range(len(halves))], x_sems)
    parts_in += bring(pieces[1:], weights[1:], w_sems.at[pl.ds(1, count - 1)])
    at = 0
    for r, parts in enumerate(halves):
        part = depth // parts
        moves[r].wait()
        for i in range(parts):
            parts_in[at].wait()
            left = x[r, :, i * part : (i + 1) * part]
            term = jnp.dot(left, branches_of(weights[at]), preferred_element_type=jnp.float32)
            if at:
                acc[...] += term
            else:
                acc[...] = term
            at += 1
    for b in range(3):
        proj_ref[b] = acc[:, b * width : (b + 1) * width].astype(jnp.bfloat16)
    for lane in range(0, width, LANES):
        lanes = slice(lane, lane + LANES)
        mix[...] = proj_ref[1, :, lanes].astype(jnp.float32) * proj_ref[2, :, lanes].astype(jnp.float32)
        gmix[...] = g_ref[:, lanes].astype(jnp.float32) * proj_ref[0, :, lanes].astype(jnp.float32)
        decay = spread(coef_ref, 0, lanes)
        long = coef_ref[2, :, lanes]
        for way, signal in enumerate((mix, gmix)):
            state = end_states(signal, slice(None), decay, run, way == 1)
            for r in range(MODES):
                runs_ref[way, lane // LANES, pl.ds(r, SUBS, stride=MODES), :] = state[r]
            total = jnp.zeros((MODES, LANES), jnp.float32)
            for i in range(SUBS):
                at = SUBS - 1 - i if way else i
                total = long * total + runs_ref[way, lane // LANES, at * MODES : (at + 1) * MODES, :]
            ends_ref[way, :, lanes] = total


def scan_kernel(run, place_ref, proj_ref, g_ref, coef_ref, skip_ref, runs_ref, ends_ref, gated_ref, gp_ref, mix, out, start):
    me = place_ref[0]
    count = ends_ref.shape[0]
    width = g_ref.shape[1]
    for lane in range(0, width, LANES):
        lanes = slice(lane, lane + LANES)
        decay = spread(coef_ref, 0, lanes)
        gain = spread(coef_ref, 1, lanes)
        long = coef_ref[2, :, lanes]
        whole = coef_ref[3, :, lanes]
        skip = skip_ref[:, lanes]
        grad = g_ref[:, lanes].astype(jnp.float32)
        query, key, value = [proj_ref[b, :, lanes].astype(jnp.float32) for b in range(3)]
        for way in range(2):
            state = jnp.zeros((MODES, LANES), jnp.float32)
            for i in range(count - 1):
                at = count - 1 - i if way else i
                keep = me < at if way else at < me
                state = jnp.where(keep, whole * state + ends_ref[at, way, :, lanes], state)
            for i in range(SUBS):
                at = SUBS - 1 - i if way else i
                start[at * MODES : (at + 1) * MODES, :] = state
                state = long * state + runs_ref[way, lane // LANES, at * MODES : (at + 1) * MODES, :]
            first = [start[pl.ds(r, SUBS, stride=MODES), :] for r in range(MODES)]
            mix[...] = grad * query if way else key * value
            full_scan(mix, out, decay, gain, first, run, way == 1)
            filtered = out[...] + skip * mix[...]
            if way:
                gp_ref[:, width + lane : width + lane + LANES] = (filtered * value).astype(jnp.bfloat16)
                gp_ref[:, 2 * width + lane : 2 * width + lane + LANES] = (filtered * key).astype(jnp.bfloat16)
            else:
                gated_ref[:, lanes] = (query * filtered).astype(jnp.bfloat16)
                gp_ref[:, lane : lane + LANES] = (grad * filtered).astype(jnp.bfloat16)


def at_rest(shape):
    return pl.BlockSpec(shape, lambda *_: (0,) * len(shape))


def away():
    return pl.BlockSpec(memory_space=pltpu.HBM)


def project(order, tokens, pieces, grad_out, coef):
    rows, inputs = tokens.shape
    width = grad_out.shape[1]
    flat = [part for piece in pieces for part in piece]
    groups = width // LANES
    return pl.pallas_call(
        functools.partial(project_kernel, rows // SUBS, [len(piece) for piece in pieces]),
        grid_spec=pltpu.PrefetchScalarGridSpec(
            num_scalar_prefetch=1,
            grid=(1,),
            in_specs=[away()] * (1 + len(flat)) + [at_rest(grad_out.shape), at_rest(coef.shape)],
            out_specs=[
                at_rest((3, rows, width)),
                at_rest((2, groups, SUBS * MODES, LANES)),
                at_rest((2, MODES, width)),
            ],
            scratch_shapes=[pltpu.VMEM(a.shape, a.dtype) for a in flat]
            + [
                pltpu.VMEM((len(pieces), rows, inputs // len(pieces)), tokens.dtype),
                pltpu.VMEM((rows, 3 * width), jnp.float32),
                pltpu.VMEM((rows, LANES), jnp.float32),
                pltpu.VMEM((rows, LANES), jnp.float32),
                pltpu.SemaphoreType.DMA((len(pieces),)),
                pltpu.SemaphoreType.DMA((len(flat),)),
            ],
        ),
        out_shape=[
            jax.ShapeDtypeStruct((3, rows, width), jnp.bfloat16),
            jax.ShapeDtypeStruct((2, groups, SUBS * MODES, LANES), jnp.float32),
            jax.ShapeDtypeStruct((2, MODES, width), jnp.float32),
        ],
        compiler_params=pltpu.CompilerParams(vmem_limit_bytes=VMEM_BYTES),
        cost_estimate=pl.CostEstimate(
            flops=2 * rows * inputs * 3 * width, bytes_accessed=2 * inputs * (rows + 3 * width), transcendentals=0
        ),
        name="project",
    )(order, tokens, *flat, grad_out, coef)


def scan(place, proj, grad_out, coef, skip, runs, ends):
    _, rows, width = proj.shape
    return pl.pallas_call(
        functools.partial(scan_kernel, rows // SUBS),
        grid_spec=pltpu.PrefetchScalarGridSpec(
            num_scalar_prefetch=1,
            grid=(1,),
            in_specs=[at_rest(a.shape) for a in (proj, grad_out, coef, skip, runs, ends)],
            out_specs=[at_rest((rows, width)), at_rest((rows, 3 * width))],
            scratch_shapes=[
                pltpu.VMEM((rows, LANES), jnp.float32),
                pltpu.VMEM((rows, LANES), jnp.float32),
                pltpu.VMEM((SUBS * MODES, LANES), jnp.float32),
            ],
        ),
        out_shape=[
            jax.ShapeDtypeStruct((rows, width), jnp.bfloat16),
            jax.ShapeDtypeStruct((rows, 3 * width), jnp.bfloat16),
        ],
        compiler_params=pltpu.CompilerParams(vmem_limit_bytes=VMEM_BYTES // 4),
        cost_estimate=pl.CostEstimate(flops=rows * width * MODES * 16, bytes_accessed=12 * rows * width, transcendentals=0),
        name="scan",
    )(place, proj, grad_out, coef, skip, runs, ends)


def input_grad_kernel(halves, core, pick_ref, *refs):
    chunks = len(halves)
    counts = [sum(h) for h in halves]
    places, total = [], 0
    for c in range(chunks):
        width = refs[c].shape[1] // 3
        places.append([slice(total + b * width, total + (b + 1) * width) for b in range(3)])
        total += 3 * width
    grads, refs = refs[:chunks], refs[chunks:]
    pieces, refs = refs[: sum(counts)], refs[sum(counts) :]
    out_ref, weights, sems = refs
    r_wanted = pick_ref[0]
    depth = weights.shape[0]
    at = 0
    for c, parts_of in enumerate(halves):
        for r, parts in enumerate(parts_of):

            @pl.when(r_wanted == r)
            def _(c=c, r=r, parts=parts, at=at):
                part = depth // parts
                for i in range(parts):
                    for b in range(3):
                        place = weights.at[i * part : (i + 1) * part, places[c][b]]
                        pltpu.make_async_copy(pieces[at + i].at[b], place, sems.at[c, b]).start()

            at += parts
    left = jnp.concatenate([g[...] for g in grads], axis=1)
    for c in range(chunks):
        for b in range(3):
            place = weights.at[:, places[c][b]]
            pltpu.make_async_copy(place, place, sems.at[c, b]).wait()
    total = lax.dot_general(left, weights[...], (((1,), (1,)), ((), ())), preferred_element_type=jnp.float32)
    out_ref[...] = total.astype(jnp.bfloat16)


def input_grad(pick, grads, weights, core):
    rows = grads[0].shape[0]
    depth = weights[0][0][0].shape[1]
    inner = sum(g.shape[1] for g in grads)
    halves = [[len(piece) for piece in pieces] for pieces in weights]
    flat = [part for pieces in weights for piece in pieces for part in piece]
    return pl.pallas_call(
        functools.partial(input_grad_kernel, halves, core),
        grid_spec=pltpu.PrefetchScalarGridSpec(
            num_scalar_prefetch=1,
            grid=(1,),
            in_specs=[at_rest(g.shape) for g in grads] + [away()] * len(flat),
            out_specs=at_rest((rows, depth)),
            scratch_shapes=[
                pltpu.VMEM((depth, inner), jnp.bfloat16),
                pltpu.SemaphoreType.DMA((len(grads), 3)),
            ],
        ),
        out_shape=jax.ShapeDtypeStruct((rows, depth), jnp.bfloat16),
        compiler_params=pltpu.CompilerParams(vmem_limit_bytes=VMEM_BYTES),
        cost_estimate=pl.CostEstimate(
            flops=2 * rows * depth * inner, bytes_accessed=2 * (inner * (rows + depth) + rows * depth), transcendentals=0
        ),
        name="input_grad",
    )(pick, *grads, *flat)


def exchange(array, axis, bit):
    count = lax.axis_size(axis)
    return lax.ppermute(array, axis, [(i, i ^ bit) for i in range(count)])


def after(value, *others):
    return lax.optimization_barrier((value, *others))[0]


class Plane:
    def __init__(self, blocks):
        self.held = []
        for c, mine in enumerate(blocks):
            if c == 1:
                mine = after(mine, self.held[0][0][0][1])
            elif c:
                mine = after(mine, self.held[c - 2][2][0][0], self.held[c - 2][4][0][0])
            far_x, far_y = exchange(mine, "seq", 2), exchange(mine, "seq", 4)
            self.held.append({0: [(mine, exchange(mine, "seq", 1))], 2: [(far_x,)], 4: [(far_y,)]})

    def relay(self, c, *gate):
        held = self.held[c]
        far_x, far_y = held[2][0][0], held[4][0][0]
        axis = far_x.ndim - 2
        half = far_x.shape[axis] // 2
        low = lax.slice_in_dim(far_x, 0, half, axis=axis)
        high = lax.slice_in_dim(far_y, half, 2 * half, axis=axis)
        gate += tuple(part[0] for part in self.held[c - 1][6]) if c else ()
        if gate:
            low, high = after((low, high), *gate)
        held[6] = [(exchange(low, "seq", 4),), (exchange(high, "seq", 2),)]

    def swap(self, c, *gate):
        for where in (2, 4, 6):
            blocks = [part[0] for part in self.held[c][where]]
            if gate:
                blocks = after(blocks, *gate)
            self.held[c][where] = [(part[0], exchange(block, "seq", 1)) for part, block in zip(self.held[c][where], blocks)]

    def pieces(self, c, places=(0, 2, 4, 6)):
        return [[pair[core] for pair in self.held[c][where]] for where in places for core in (0, 1)]


def gather_whole(mine):
    whole = lax.all_gather(mine, "seq", axis=1, tiled=True)
    return [[piece] for piece in jnp.split(whole, BLOCKS, axis=1)]


def local(tokens, proj_weight, residues, decay_rates, skip_gain, grad_out):
    rows = tokens.shape[0]
    depth = proj_weight.shape[0]
    channels = skip_gain.shape[0]
    groups = lax.axis_size("chan")
    me = lax.axis_index("seq").astype(jnp.int32)
    z = lax.axis_index("chan").astype(jnp.int32)
    direct = lax.axis_size("seq") == BLOCKS and groups == 4
    order = jnp.arange(BLOCKS, dtype=jnp.int32)
    if direct:
        order = order ^ me
    coef = coefficients(residues, decay_rates, rows)
    skip = skip_gain[None, :]
    branches = proj_weight.swapaxes(0, 1)
    slots, first = [], 0
    while first < channels:
        width = WIDTHS[min(len(slots), len(WIDTHS) - 1)]
        slots.append(slice(first, first + width))
        first += width
    chunks = len(slots)
    mine = [branches[:, :, lanes] for lanes in slots]

    def forward(c, pieces):
        lanes = slots[c]
        return project(order, tokens, pieces, grad_out[:, lanes], coef[:, :, lanes])

    def middle(span, made):
        ends = lax.all_gather(jnp.concatenate([m[2] for m in made], axis=2), "seq")
        gated, grads = [], []
        start = slots[span[0]].start
        for i, c in enumerate(span):
            lanes = slots[c]
            proj, runs, _ = made[i]
            seen = ends[:, :, :, lanes.start - start : lanes.stop - start]
            gate, grad = scan(me.reshape(1), proj, grad_out[:, lanes], coef[:, :, lanes], skip[:, lanes], runs, seen)
            gated.append(gate)
            grads.append(grad)
        return gated, grads

    if not direct:
        weights = [gather_whole(a) for a in mine]
        made = [forward(c, weights[c]) for c in range(chunks)]
        gated, grads = middle(range(chunks), made)
        flat = [jnp.concatenate([p[0][b] for p in pieces], axis=0) for pieces in weights for b in range(3)]
        contract = (((1,), (1,)), ((), ()))
        dx = lax.dot_general(jnp.concatenate(grads, axis=1), jnp.concatenate(flat, axis=1), contract, preferred_element_type=jnp.float32)
        grad_tokens = lax.psum_scatter(dx.astype(jnp.bfloat16), "chan", scatter_dimension=1, tiled=True)
        return (jnp.concatenate(gated, axis=1), grad_tokens)

    plane = Plane(mine)
    plane.relay(0)
    plane.swap(0)
    made = [forward(0, plane.pieces(0))]
    plane.relay(1)
    plane.swap(1, made[0][2])
    plane.relay(2, made[0][2])
    made.append(forward(1, plane.pieces(1)))
    plane.swap(2, made[1][2])
    made.append(forward(2, plane.pieces(2)))
    gated, grads = middle(range(chunks), made)
    weights = [plane.pieces(c) for c in range(chunks)]

    turns = jnp.array([[3, 2, 1, 0], [3, 2, 0, 1], [0, 1, 3, 2], [0, 1, 2, 3]], jnp.int32)[z]
    inwards, across, outwards = [(0, 1), (3, 2)], [(1, 2), (2, 1)], [(1, 0), (2, 3)]

    def part(turn, core):
        pick = me ^ (2 * turns[turn] + core)
        return input_grad(pick.reshape(1), grads, weights, core)

    def add(*terms):
        return sum(t.astype(jnp.float32) for t in terms).astype(jnp.bfloat16)

    sent = []

    def send(block, pairs):
        return lax.ppermute(block, "chan", pairs)

    parts = [[None, None] for _ in range(4)]
    got = [[None, None] for _ in range(3)]
    swapped = [[None, None] for _ in range(3)]
    for turn in range(3):
        for core in range(2):
            parts[turn][core] = part(turn, core)
            block = parts[turn][core]
            if len(sent) >= 2:
                block = after(block, sent[-2])
            got[turn][core] = send(block, inwards)
            sent.append(got[turn][core])
            if turn:
                swapped[turn][core] = send(add(parts[turn - 1][core], got[turn - 1][core]), across)
    out = []
    for core in range(2):
        last = part(3, core)
        back = send(add(parts[2][core], swapped[1][core]), outwards)
        out.append(add(last, got[2][core], swapped[2][core], back))
    return (jnp.concatenate(gated, axis=1), jnp.concatenate(out, axis=1))


def solution(mesh):
    placed = (
        P("seq", None),
        P("seq", None, "chan"),
        P(None, "chan"),
        P(None, "chan"),
        P("chan"),
        P("seq", "chan"),
    )
    return jax.shard_map(
        local,
        mesh=mesh,
        in_specs=placed,
        out_specs=(P("seq", "chan"), P("seq", "chan")),
        check_vma=False,
    )
```

```python
import functools

import jax
import jax.numpy as jnp
from jax import lax
from jax.experimental import pallas as pl
from jax.experimental.pallas import tpu as pltpu
from jax.sharding import PartitionSpec as P

LANES = 128
WIDTHS = (256, 256)
SUBS = 8
MODES = 16
BLOCKS = 8
VMEM_BYTES = 60 * 1024 * 1024


def coefficients(residues, decay_rates, rows):
    return jnp.stack(
        [
            jnp.exp(-decay_rates),
            residues * jnp.sqrt(-jnp.expm1(-2.0 * decay_rates)),
            jnp.exp(-decay_rates * (rows // SUBS)),
            jnp.exp(-decay_rates * rows),
        ]
    )


def spread(coef_ref, which, lanes):
    table = coef_ref[which, :, lanes]
    return [jnp.broadcast_to(table[r : r + 1, :], (SUBS, LANES)) for r in range(MODES)]


def end_states(signal_ref, lanes, decay, run, backward):
    def step(j, state):
        at = run - 1 - j if backward else j
        row = signal_ref[pl.ds(at, SUBS, stride=run), lanes]
        return tuple(a * s + row for a, s in zip(decay, state))

    zero = jnp.zeros((SUBS, LANES), jnp.float32)
    return lax.fori_loop(0, run, step, (zero,) * MODES, unroll=8)


def full_scan(signal_ref, out_ref, decay, gain, state, run, backward):
    def step(j, state):
        at = run - 1 - j if backward else j
        rows = pl.ds(at, SUBS, stride=run)
        row = signal_ref[rows, :]
        state = tuple(a * s + row for a, s in zip(decay, state))
        terms = [g * s for g, s in zip(gain, state)]
        while len(terms) > 1:
            terms = [terms[i] + terms[i + 1] for i in range(0, len(terms), 2)]
        out_ref[rows, :] = terms[0]
        return state

    lax.fori_loop(0, run, step, tuple(state), unroll=8)


def bring(sources, targets, sems):
    copies = [pltpu.make_async_copy(a, b, sems.at[i]) for i, (a, b) in enumerate(zip(sources, targets))]
    for copy in copies:
        copy.start()
    return copies


def product(order_ref, x_ref, pieces, halves, x, w, x_sems, w_sems):
    depth = x.shape[2]
    width = w.shape[2] // 3
    loads, at = [], 0
    for r, parts in enumerate(halves):
        columns = pl.ds(pl.multiple_of(order_ref[r] * depth, depth), depth)
        load = bring([x_ref.at[:, columns]], [x.at[r]], x_sems.at[pl.ds(r, 1)])
        part = depth // parts
        for i in range(parts):
            targets = [w.at[r, pl.ds(i * part, part), pl.ds(b * width, width)] for b in range(3)]
            load += bring([pieces[at].at[b] for b in range(3)], targets, w_sems.at[at])
            at += 1
        loads.append(load)
    total = None
    for r in range(len(halves)):
        for copy in loads[r]:
            copy.wait()
        term = jnp.dot(x[r], w[r], preferred_element_type=jnp.float32)
        total = term if total is None else total + term
    return total


def project_part_kernel(halves, order_ref, x_ref, *refs):
    count = sum(halves)
    pieces, (out_ref, x, w, x_sems, w_sems) = refs[:count], refs[count:]
    out_ref[...] = product(order_ref, x_ref, pieces, halves, x, w, x_sems, w_sems)


def project_kernel(run, halves, order_ref, x_ref, *refs):
    count = sum(halves)
    pieces, refs = refs[:count], refs[count:]
    part_ref, g_ref, coef_ref, proj_ref, runs_ref, ends_ref, x, w, mix, gmix, x_sems, w_sems = refs
    width = g_ref.shape[1]
    total = part_ref[...] + product(order_ref, x_ref, pieces, halves, x, w, x_sems, w_sems)
    for b in range(3):
        proj_ref[b] = total[:, b * width : (b + 1) * width].astype(jnp.bfloat16)
    for lane in range(0, width, LANES):
        lanes = slice(lane, lane + LANES)
        mix[...] = proj_ref[1, :, lanes].astype(jnp.float32) * proj_ref[2, :, lanes].astype(jnp.float32)
        gmix[...] = g_ref[:, lanes].astype(jnp.float32) * proj_ref[0, :, lanes].astype(jnp.float32)
        decay = spread(coef_ref, 0, lanes)
        long = coef_ref[2, :, lanes]
        for way, signal in enumerate((mix, gmix)):
            state = end_states(signal, slice(None), decay, run, way == 1)
            for r in range(MODES):
                runs_ref[way, lane // LANES, pl.ds(r, SUBS, stride=MODES), :] = state[r]
            total = jnp.zeros((MODES, LANES), jnp.float32)
            for i in range(SUBS):
                at = SUBS - 1 - i if way else i
                total = long * total + runs_ref[way, lane // LANES, at * MODES : (at + 1) * MODES, :]
            ends_ref[way, :, lanes] = total


def scan_kernel(run, place_ref, proj_ref, g_ref, coef_ref, skip_ref, runs_ref, ends_ref, gated_ref, gp_ref, mix, out, start):
    me = place_ref[0]
    count = ends_ref.shape[0]
    width = g_ref.shape[1]
    for lane in range(0, width, LANES):
        lanes = slice(lane, lane + LANES)
        decay = spread(coef_ref, 0, lanes)
        gain = spread(coef_ref, 1, lanes)
        long = coef_ref[2, :, lanes]
        whole = coef_ref[3, :, lanes]
        skip = skip_ref[:, lanes]
        grad = g_ref[:, lanes].astype(jnp.float32)
        query, key, value = [proj_ref[b, :, lanes].astype(jnp.float32) for b in range(3)]
        for way in range(2):
            state = jnp.zeros((MODES, LANES), jnp.float32)
            for i in range(count - 1):
                at = count - 1 - i if way else i
                keep = me < at if way else at < me
                state = jnp.where(keep, whole * state + ends_ref[at, way, :, lanes], state)
            for i in range(SUBS):
                at = SUBS - 1 - i if way else i
                start[at * MODES : (at + 1) * MODES, :] = state
                state = long * state + runs_ref[way, lane // LANES, at * MODES : (at + 1) * MODES, :]
            first = [start[pl.ds(r, SUBS, stride=MODES), :] for r in range(MODES)]
            mix[...] = grad * query if way else key * value
            full_scan(mix, out, decay, gain, first, run, way == 1)
            filtered = out[...] + skip * mix[...]
            if way:
                gp_ref[:, width + lane : width + lane + LANES] = (filtered * value).astype(jnp.bfloat16)
                gp_ref[:, 2 * width + lane : 2 * width + lane + LANES] = (filtered * key).astype(jnp.bfloat16)
            else:
                gated_ref[:, lanes] = (query * filtered).astype(jnp.bfloat16)
                gp_ref[:, lane : lane + LANES] = (grad * filtered).astype(jnp.bfloat16)


def at_rest(shape):
    return pl.BlockSpec(shape, lambda *_: (0,) * len(shape))


def away():
    return pl.BlockSpec(memory_space=pltpu.HBM)


def block_scratch(tokens, pieces, width):
    rows, inputs = tokens.shape
    depth = inputs // BLOCKS
    parts = [len(piece) for piece in pieces]
    buffers = [
        pltpu.VMEM((len(pieces), rows, depth), tokens.dtype),
        pltpu.VMEM((len(pieces), depth, 3 * width), tokens.dtype),
    ]
    return parts, buffers, [pltpu.SemaphoreType.DMA((len(pieces),)), pltpu.SemaphoreType.DMA((sum(parts), 3))]


def product_cost(tokens, pieces, width):
    rows = tokens.shape[0]
    depth = tokens.shape[1] // BLOCKS * len(pieces)
    return pl.CostEstimate(
        flops=2 * rows * depth * 3 * width, bytes_accessed=2 * depth * (rows + 3 * width), transcendentals=0
    )


def project_part(order, tokens, pieces):
    rows = tokens.shape[0]
    flat = [part for piece in pieces for part in piece]
    width = flat[0].shape[2]
    halves, buffers, sems = block_scratch(tokens, pieces, width)
    return pl.pallas_call(
        functools.partial(project_part_kernel, halves),
        grid_spec=pltpu.PrefetchScalarGridSpec(
            num_scalar_prefetch=1,
            grid=(1,),
            in_specs=[away()] * (1 + len(flat)),
            out_specs=at_rest((rows, 3 * width)),
            scratch_shapes=buffers + sems,
        ),
        out_shape=jax.ShapeDtypeStruct((rows, 3 * width), jnp.float32),
        compiler_params=pltpu.CompilerParams(vmem_limit_bytes=VMEM_BYTES),
        cost_estimate=product_cost(tokens, pieces, width),
        name="project_part",
    )(order, tokens, *flat)


def project(order, tokens, pieces, part, grad_out, coef):
    rows = tokens.shape[0]
    width = grad_out.shape[1]
    flat = [part for piece in pieces for part in piece]
    groups = width // LANES
    halves, buffers, sems = block_scratch(tokens, pieces, width)
    return pl.pallas_call(
        functools.partial(project_kernel, rows // SUBS, halves),
        grid_spec=pltpu.PrefetchScalarGridSpec(
            num_scalar_prefetch=1,
            grid=(1,),
            in_specs=[away()] * (1 + len(flat)) + [at_rest(a.shape) for a in (part, grad_out, coef)],
            out_specs=[
                at_rest((3, rows, width)),
                at_rest((2, groups, SUBS * MODES, LANES)),
                at_rest((2, MODES, width)),
            ],
            scratch_shapes=buffers
            + [
                pltpu.VMEM((rows, LANES), jnp.float32),
                pltpu.VMEM((rows, LANES), jnp.float32),
            ]
            + sems,
        ),
        out_shape=[
            jax.ShapeDtypeStruct((3, rows, width), jnp.bfloat16),
            jax.ShapeDtypeStruct((2, groups, SUBS * MODES, LANES), jnp.float32),
            jax.ShapeDtypeStruct((2, MODES, width), jnp.float32),
        ],
        compiler_params=pltpu.CompilerParams(vmem_limit_bytes=VMEM_BYTES),
        cost_estimate=product_cost(tokens, pieces, width),
        name="project",
    )(order, tokens, *flat, part, grad_out, coef)


def scan(place, proj, grad_out, coef, skip, runs, ends):
    _, rows, width = proj.shape
    return pl.pallas_call(
        functools.partial(scan_kernel, rows // SUBS),
        grid_spec=pltpu.PrefetchScalarGridSpec(
            num_scalar_prefetch=1,
            grid=(1,),
            in_specs=[at_rest(a.shape) for a in (proj, grad_out, coef, skip, runs, ends)],
            out_specs=[at_rest((rows, width)), at_rest((rows, 3 * width))],
            scratch_shapes=[
                pltpu.VMEM((rows, LANES), jnp.float32),
                pltpu.VMEM((rows, LANES), jnp.float32),
                pltpu.VMEM((SUBS * MODES, LANES), jnp.float32),
            ],
        ),
        out_shape=[
            jax.ShapeDtypeStruct((rows, width), jnp.bfloat16),
            jax.ShapeDtypeStruct((rows, 3 * width), jnp.bfloat16),
        ],
        compiler_params=pltpu.CompilerParams(vmem_limit_bytes=VMEM_BYTES // 4),
        cost_estimate=pl.CostEstimate(flops=rows * width * MODES * 16, bytes_accessed=12 * rows * width, transcendentals=0),
        name="scan",
    )(place, proj, grad_out, coef, skip, runs, ends)


def input_grad_kernel(halves, core, pick_ref, *refs):
    chunks = len(halves)
    counts = [sum(h) for h in halves]
    places, total = [], 0
    for c in range(chunks):
        width = refs[c].shape[1] // 3
        places.append([slice(total + b * width, total + (b + 1) * width) for b in range(3)])
        total += 3 * width
    grads, refs = refs[:chunks], refs[chunks:]
    pieces, refs = refs[: sum(counts)], refs[sum(counts) :]
    out_ref, weights, sems = refs
    r_wanted = pick_ref[0]
    depth = weights.shape[0]
    at = 0
    for c, parts_of in enumerate(halves):
        for r, parts in enumerate(parts_of):

            @pl.when(r_wanted == r)
            def _(c=c, r=r, parts=parts, at=at):
                part = depth // parts
                for i in range(parts):
                    for b in range(3):
                        place = weights.at[i * part : (i + 1) * part, places[c][b]]
                        pltpu.make_async_copy(pieces[at + i].at[b], place, sems.at[c, b]).start()

            at += parts
    left = jnp.concatenate([g[...] for g in grads], axis=1)
    for c in range(chunks):
        for b in range(3):
            place = weights.at[:, places[c][b]]
            pltpu.make_async_copy(place, place, sems.at[c, b]).wait()
    total = lax.dot_general(left, weights[...], (((1,), (1,)), ((), ())), preferred_element_type=jnp.float32)
    out_ref[...] = total.astype(jnp.bfloat16)


def input_grad(pick, grads, weights, core):
    rows = grads[0].shape[0]
    depth = weights[0][0][0].shape[1]
    inner = sum(g.shape[1] for g in grads)
    halves = [[len(piece) for piece in pieces] for pieces in weights]
    flat = [part for pieces in weights for piece in pieces for part in piece]
    return pl.pallas_call(
        functools.partial(input_grad_kernel, halves, core),
        grid_spec=pltpu.PrefetchScalarGridSpec(
            num_scalar_prefetch=1,
            grid=(1,),
            in_specs=[at_rest(g.shape) for g in grads] + [away()] * len(flat),
            out_specs=at_rest((rows, depth)),
            scratch_shapes=[
                pltpu.VMEM((depth, inner), jnp.bfloat16),
                pltpu.SemaphoreType.DMA((len(grads), 3)),
            ],
        ),
        out_shape=jax.ShapeDtypeStruct((rows, depth), jnp.bfloat16),
        compiler_params=pltpu.CompilerParams(vmem_limit_bytes=VMEM_BYTES),
        cost_estimate=pl.CostEstimate(
            flops=2 * rows * depth * inner, bytes_accessed=2 * (inner * (rows + depth) + rows * depth), transcendentals=0
        ),
        name="input_grad",
    )(pick, *grads, *flat)


def exchange(array, axis, bit):
    count = lax.axis_size(axis)
    return lax.ppermute(array, axis, [(i, i ^ bit) for i in range(count)])


def after(value, *others):
    return lax.optimization_barrier((value, *others))[0]


class Plane:
    def __init__(self, blocks):
        self.blocks = blocks
        self.held = [{} for _ in blocks]

    def own(self, c, *gate):
        mine = after(self.blocks[c], *gate) if gate else self.blocks[c]
        self.held[c][2] = [(exchange(mine, "seq", 2),)]
        self.held[c][4] = [(exchange(mine, "seq", 4),)]
        self.held[c][0] = [(mine, exchange(mine, "seq", 1))]

    def came(self, c, *places):
        return [part[0] for where in places for part in self.held[c][where]]

    def swapped(self, c, *places):
        return [part[1] for where in places for part in self.held[c][where]]

    def relay(self, c, *gate):
        far_x, far_y = self.came(c, 2, 4)
        axis = far_x.ndim - 2
        half = far_x.shape[axis] // 2
        low = lax.slice_in_dim(far_x, 0, half, axis=axis)
        high = lax.slice_in_dim(far_y, half, 2 * half, axis=axis)
        if gate:
            low, high = after((low, high), *gate)
        self.held[c][6] = [(exchange(low, "seq", 4),), (exchange(high, "seq", 2),)]

    def swap(self, c, places, *gate):
        for where in places:
            blocks = self.came(c, where)
            if gate:
                blocks = after(blocks, *gate)
            self.held[c][where] = [(part[0], exchange(block, "seq", 1)) for part, block in zip(self.held[c][where], blocks)]

    def pieces(self, c, places=(0, 2, 4, 6)):
        return [[pair[core] for pair in self.held[c][where]] for where in places for core in (0, 1)]


def gather_whole(mine):
    whole = lax.all_gather(mine, "seq", axis=1, tiled=True)
    return [[piece] for piece in jnp.split(whole, BLOCKS, axis=1)]


def local(tokens, proj_weight, residues, decay_rates, skip_gain, grad_out):
    rows = tokens.shape[0]
    depth = proj_weight.shape[0]
    channels = skip_gain.shape[0]
    groups = lax.axis_size("chan")
    me = lax.axis_index("seq").astype(jnp.int32)
    z = lax.axis_index("chan").astype(jnp.int32)
    direct = lax.axis_size("seq") == BLOCKS and groups == 4
    order = jnp.arange(BLOCKS, dtype=jnp.int32)
    if direct:
        order = order ^ me
    coef = coefficients(residues, decay_rates, rows)
    skip = skip_gain[None, :]
    branches = proj_weight.swapaxes(0, 1)
    slots, first = [], 0
    while first < channels:
        width = WIDTHS[min(len(slots), len(WIDTHS) - 1)]
        slots.append(slice(first, first + width))
        first += width
    chunks = len(slots)
    mine = [branches[:, :, lanes] for lanes in slots]

    def forward(c, pieces, part):
        lanes = slots[c]
        count = len(pieces)
        return project(order[BLOCKS - count :], tokens, pieces, part, grad_out[:, lanes], coef[:, :, lanes])

    def meet(made):
        return lax.all_gather(jnp.concatenate([m[2] for m in made], axis=2), "seq")

    def scans(span, made, seen):
        gated, grads = [], []
        start = slots[span[0]].start
        for i, c in enumerate(span):
            lanes = slots[c]
            proj, runs, _ = made[i]
            ends = seen[:, :, :, lanes.start - start : lanes.stop - start]
            gate, grad = scan(me.reshape(1), proj, grad_out[:, lanes], coef[:, :, lanes], skip[:, lanes], runs, ends)
            gated.append(gate)
            grads.append(grad)
        return gated, grads

    if not direct:
        weights = [gather_whole(a) for a in mine]
        made = []
        for c in range(chunks):
            part = project_part(order[:6], tokens, weights[c][:6])
            made.append(forward(c, weights[c][6:], part))
        gated, grads = scans(range(chunks), made, meet(made))
        flat = [jnp.concatenate([p[0][b] for p in pieces], axis=0) for pieces in weights for b in range(3)]
        contract = (((1,), (1,)), ((), ()))
        dx = lax.dot_general(jnp.concatenate(grads, axis=1), jnp.concatenate(flat, axis=1), contract, preferred_element_type=jnp.float32)
        grad_tokens = lax.psum_scatter(dx.astype(jnp.bfloat16), "chan", scatter_dimension=1, tiled=True)
        return (jnp.concatenate(gated, axis=1), grad_tokens)

    plane = Plane(mine)
    near, far = (0, 2, 4), (6,)
    plane.own(0)
    plane.relay(0)
    plane.swap(0, (2, 4))
    plane.own(1, *plane.swapped(0, 0, 2, 4))
    plane.swap(0, far)
    part = project_part(order[:6], tokens, plane.pieces(0, near))
    made = [forward(0, plane.pieces(0, far), part)]
    seen = meet(made)
    plane.relay(1, seen)
    plane.swap(1, (2, 4), seen)
    gated, grads = scans((0,), made, seen)
    part = project_part(order[:6], tokens, plane.pieces(1, near))
    plane.swap(1, far, part, grads[0])
    made.append(forward(1, plane.pieces(1, far), part))
    late = scans((1,), made[1:], meet(made[1:]))
    gated, grads = gated + late[0], grads + late[1]
    weights = [plane.pieces(c) for c in range(chunks)]

    turns = jnp.array([[3, 2, 1, 0], [3, 2, 0, 1], [0, 1, 3, 2], [0, 1, 2, 3]], jnp.int32)[z]
    inwards, across, outwards = [(0, 1), (3, 2)], [(1, 2), (2, 1)], [(1, 0), (2, 3)]

    def part(turn, core):
        pick = me ^ (2 * turns[turn] + core)
        return input_grad(pick.reshape(1), grads, weights, core)

    def add(*terms):
        return sum(t.astype(jnp.float32) for t in terms).astype(jnp.bfloat16)

    sent = []

    def send(block, pairs):
        return lax.ppermute(block, "chan", pairs)

    parts = [[None, None] for _ in range(4)]
    got = [[None, None] for _ in range(3)]
    swapped = [[None, None] for _ in range(3)]
    for turn in range(3):
        for core in range(2):
            parts[turn][core] = part(turn, core)
            block = parts[turn][core]
            if len(sent) >= 2:
                block = after(block, sent[-2])
            got[turn][core] = send(block, inwards)
            sent.append(got[turn][core])
            if turn:
                swapped[turn][core] = send(add(parts[turn - 1][core], got[turn - 1][core]), across)
    out = []
    for core in range(2):
        last = part(3, core)
        back = send(add(parts[2][core], swapped[1][core]), outwards)
        out.append(add(last, got[2][core], swapped[2][core], back))
    return (jnp.concatenate(gated, axis=1), jnp.concatenate(out, axis=1))


def solution(mesh):
    placed = (
        P("seq", None),
        P("seq", None, "chan"),
        P(None, "chan"),
        P(None, "chan"),
        P("chan"),
        P("seq", "chan"),
    )
    return jax.shard_map(
        local,
        mesh=mesh,
        in_specs=placed,
        out_specs=(P("seq", "chan"), P("seq", "chan")),
        check_vma=False,
    )
```

```python
import functools

import jax
import jax.numpy as jnp
from jax import lax
from jax.experimental import pallas as pl
from jax.experimental.pallas import tpu as pltpu
from jax.sharding import PartitionSpec as P

LANES = 128
WIDTHS = (256, 256)
SUBS = 8
MODES = 16
BLOCKS = 8
VMEM_BYTES = 60 * 1024 * 1024


def coefficients(residues, decay_rates, rows):
    return jnp.stack(
        [
            jnp.exp(-decay_rates),
            residues * jnp.sqrt(-jnp.expm1(-2.0 * decay_rates)),
            jnp.exp(-decay_rates * (rows // SUBS)),
            jnp.exp(-decay_rates * rows),
        ]
    )


def spread(coef_ref, which, lanes):
    table = coef_ref[which, :, lanes]
    return [jnp.broadcast_to(table[r : r + 1, :], (SUBS, LANES)) for r in range(MODES)]


def end_states(signal_ref, lanes, decay, run, backward):
    def step(j, state):
        at = run - 1 - j if backward else j
        row = signal_ref[pl.ds(at, SUBS, stride=run), lanes]
        return tuple(a * s + row for a, s in zip(decay, state))

    zero = jnp.zeros((SUBS, LANES), jnp.float32)
    return lax.fori_loop(0, run, step, (zero,) * MODES, unroll=8)


def full_scan(signal_ref, out_ref, decay, gain, state, run, backward):
    def step(j, state):
        at = run - 1 - j if backward else j
        rows = pl.ds(at, SUBS, stride=run)
        row = signal_ref[rows, :]
        state = tuple(a * s + row for a, s in zip(decay, state))
        terms = [g * s for g, s in zip(gain, state)]
        while len(terms) > 1:
            terms = [terms[i] + terms[i + 1] for i in range(0, len(terms), 2)]
        out_ref[rows, :] = terms[0]
        return state

    lax.fori_loop(0, run, step, tuple(state), unroll=8)


def bring(sources, targets, sems):
    copies = [pltpu.make_async_copy(a, b, sems.at[i]) for i, (a, b) in enumerate(zip(sources, targets))]
    for copy in copies:
        copy.start()
    return copies


def product(order_ref, x_ref, pieces, halves, x, w, x_sems, w_sems):
    depth = x.shape[2]
    width = w.shape[2] // 3
    loads, at = [], 0
    for r, parts in enumerate(halves):
        columns = pl.ds(pl.multiple_of(order_ref[r] * depth, depth), depth)
        load = bring([x_ref.at[:, columns]], [x.at[r]], x_sems.at[pl.ds(r, 1)])
        part = depth // parts
        for i in range(parts):
            targets = [w.at[r, pl.ds(i * part, part), pl.ds(b * width, width)] for b in range(3)]
            load += bring([pieces[at].at[b] for b in range(3)], targets, w_sems.at[at])
            at += 1
        loads.append(load)
    total = None
    for r in range(len(halves)):
        for copy in loads[r]:
            copy.wait()
        term = jnp.dot(x[r], w[r], preferred_element_type=jnp.float32)
        total = term if total is None else total + term
    return total


def project_part_kernel(halves, order_ref, x_ref, *refs):
    count = sum(halves)
    pieces, (out_ref, x, w, x_sems, w_sems) = refs[:count], refs[count:]
    out_ref[...] = product(order_ref, x_ref, pieces, halves, x, w, x_sems, w_sems)


def project_kernel(run, halves, order_ref, x_ref, *refs):
    count = sum(halves)
    pieces, refs = refs[:count], refs[count:]
    part_ref, g_ref, coef_ref, proj_ref, runs_ref, ends_ref, x, w, mix, gmix, x_sems, w_sems = refs
    width = g_ref.shape[1]
    total = part_ref[...] + product(order_ref, x_ref, pieces, halves, x, w, x_sems, w_sems)
    for b in range(3):
        proj_ref[b] = total[:, b * width : (b + 1) * width].astype(jnp.bfloat16)
    for lane in range(0, width, LANES):
        lanes = slice(lane, lane + LANES)
        mix[...] = proj_ref[1, :, lanes].astype(jnp.float32) * proj_ref[2, :, lanes].astype(jnp.float32)
        gmix[...] = g_ref[:, lanes].astype(jnp.float32) * proj_ref[0, :, lanes].astype(jnp.float32)
        decay = spread(coef_ref, 0, lanes)
        long = coef_ref[2, :, lanes]
        for way, signal in enumerate((mix, gmix)):
            state = end_states(signal, slice(None), decay, run, way == 1)
            for r in range(MODES):
                runs_ref[way, lane // LANES, pl.ds(r, SUBS, stride=MODES), :] = state[r]
            total = jnp.zeros((MODES, LANES), jnp.float32)
            for i in range(SUBS):
                at = SUBS - 1 - i if way else i
                total = long * total + runs_ref[way, lane // LANES, at * MODES : (at + 1) * MODES, :]
            ends_ref[way, :, lanes] = total


def scan_kernel(run, place_ref, proj_ref, g_ref, coef_ref, skip_ref, runs_ref, ends_ref, gated_ref, gp_ref, mix, out, start):
    me = place_ref[0]
    count = ends_ref.shape[0]
    width = g_ref.shape[1]
    for lane in range(0, width, LANES):
        lanes = slice(lane, lane + LANES)
        decay = spread(coef_ref, 0, lanes)
        gain = spread(coef_ref, 1, lanes)
        long = coef_ref[2, :, lanes]
        whole = coef_ref[3, :, lanes]
        skip = skip_ref[:, lanes]
        grad = g_ref[:, lanes].astype(jnp.float32)
        query, key, value = [proj_ref[b, :, lanes].astype(jnp.float32) for b in range(3)]
        for way in range(2):
            state = jnp.zeros((MODES, LANES), jnp.float32)
            for i in range(count - 1):
                at = count - 1 - i if way else i
                keep = me < at if way else at < me
                state = jnp.where(keep, whole * state + ends_ref[at, way, :, lanes], state)
            for i in range(SUBS):
                at = SUBS - 1 - i if way else i
                start[at * MODES : (at + 1) * MODES, :] = state
                state = long * state + runs_ref[way, lane // LANES, at * MODES : (at + 1) * MODES, :]
            first = [start[pl.ds(r, SUBS, stride=MODES), :] for r in range(MODES)]
            mix[...] = grad * query if way else key * value
            full_scan(mix, out, decay, gain, first, run, way == 1)
            filtered = out[...] + skip * mix[...]
            if way:
                gp_ref[:, width + lane : width + lane + LANES] = (filtered * value).astype(jnp.bfloat16)
                gp_ref[:, 2 * width + lane : 2 * width + lane + LANES] = (filtered * key).astype(jnp.bfloat16)
            else:
                gated_ref[:, lanes] = (query * filtered).astype(jnp.bfloat16)
                gp_ref[:, lane : lane + LANES] = (grad * filtered).astype(jnp.bfloat16)


def at_rest(shape):
    return pl.BlockSpec(shape, lambda *_: (0,) * len(shape))


def away():
    return pl.BlockSpec(memory_space=pltpu.HBM)


def block_scratch(tokens, pieces, width):
    rows, inputs = tokens.shape
    depth = inputs // BLOCKS
    parts = [len(piece) for piece in pieces]
    buffers = [
        pltpu.VMEM((len(pieces), rows, depth), tokens.dtype),
        pltpu.VMEM((len(pieces), depth, 3 * width), tokens.dtype),
    ]
    return parts, buffers, [pltpu.SemaphoreType.DMA((len(pieces),)), pltpu.SemaphoreType.DMA((sum(parts), 3))]


def product_cost(tokens, pieces, width):
    rows = tokens.shape[0]
    depth = tokens.shape[1] // BLOCKS * len(pieces)
    return pl.CostEstimate(
        flops=2 * rows * depth * 3 * width, bytes_accessed=2 * depth * (rows + 3 * width), transcendentals=0
    )


def project_part(order, tokens, pieces):
    rows = tokens.shape[0]
    flat = [part for piece in pieces for part in piece]
    width = flat[0].shape[2]
    halves, buffers, sems = block_scratch(tokens, pieces, width)
    return pl.pallas_call(
        functools.partial(project_part_kernel, halves),
        grid_spec=pltpu.PrefetchScalarGridSpec(
            num_scalar_prefetch=1,
            grid=(1,),
            in_specs=[away()] * (1 + len(flat)),
            out_specs=at_rest((rows, 3 * width)),
            scratch_shapes=buffers + sems,
        ),
        out_shape=jax.ShapeDtypeStruct((rows, 3 * width), jnp.float32),
        compiler_params=pltpu.CompilerParams(vmem_limit_bytes=32 * 1024 * 1024),
        cost_estimate=product_cost(tokens, pieces, width),
        name="project_part",
    )(order, tokens, *flat)


def project(order, tokens, pieces, part, grad_out, coef):
    rows = tokens.shape[0]
    width = grad_out.shape[1]
    flat = [part for piece in pieces for part in piece]
    groups = width // LANES
    halves, buffers, sems = block_scratch(tokens, pieces, width)
    return pl.pallas_call(
        functools.partial(project_kernel, rows // SUBS, halves),
        grid_spec=pltpu.PrefetchScalarGridSpec(
            num_scalar_prefetch=1,
            grid=(1,),
            in_specs=[away()] * (1 + len(flat)) + [at_rest(a.shape) for a in (part, grad_out, coef)],
            out_specs=[
                at_rest((3, rows, width)),
                at_rest((2, groups, SUBS * MODES, LANES)),
                at_rest((2, MODES, width)),
            ],
            scratch_shapes=buffers
            + [
                pltpu.VMEM((rows, LANES), jnp.float32),
                pltpu.VMEM((rows, LANES), jnp.float32),
            ]
            + sems,
        ),
        out_shape=[
            jax.ShapeDtypeStruct((3, rows, width), jnp.bfloat16),
            jax.ShapeDtypeStruct((2, groups, SUBS * MODES, LANES), jnp.float32),
            jax.ShapeDtypeStruct((2, MODES, width), jnp.float32),
        ],
        compiler_params=pltpu.CompilerParams(vmem_limit_bytes=16 * 1024 * 1024),
        cost_estimate=product_cost(tokens, pieces, width),
        name="project",
    )(order, tokens, *flat, part, grad_out, coef)


def scan(place, proj, grad_out, coef, skip, runs, ends):
    _, rows, width = proj.shape
    return pl.pallas_call(
        functools.partial(scan_kernel, rows // SUBS),
        grid_spec=pltpu.PrefetchScalarGridSpec(
            num_scalar_prefetch=1,
            grid=(1,),
            in_specs=[at_rest(a.shape) for a in (proj, grad_out, coef, skip, runs, ends)],
            out_specs=[at_rest((rows, width)), at_rest((rows, 3 * width))],
            scratch_shapes=[
                pltpu.VMEM((rows, LANES), jnp.float32),
                pltpu.VMEM((rows, LANES), jnp.float32),
                pltpu.VMEM((SUBS * MODES, LANES), jnp.float32),
            ],
        ),
        out_shape=[
            jax.ShapeDtypeStruct((rows, width), jnp.bfloat16),
            jax.ShapeDtypeStruct((rows, 3 * width), jnp.bfloat16),
        ],
        compiler_params=pltpu.CompilerParams(vmem_limit_bytes=VMEM_BYTES // 4),
        cost_estimate=pl.CostEstimate(flops=rows * width * MODES * 16, bytes_accessed=12 * rows * width, transcendentals=0),
        name="scan",
    )(place, proj, grad_out, coef, skip, runs, ends)


def input_grad_kernel(halves, core, pick_ref, *refs):
    chunks = len(halves)
    counts = [sum(h) for h in halves]
    places, total = [], 0
    for c in range(chunks):
        width = refs[c].shape[1] // 3
        places.append([slice(total + b * width, total + (b + 1) * width) for b in range(3)])
        total += 3 * width
    grads, refs = refs[:chunks], refs[chunks:]
    pieces, refs = refs[: sum(counts)], refs[sum(counts) :]
    out_ref, weights, sems = refs
    r_wanted = pick_ref[0]
    depth = weights.shape[0]
    at = 0
    for c, parts_of in enumerate(halves):
        for r, parts in enumerate(parts_of):

            @pl.when(r_wanted == r)
            def _(c=c, r=r, parts=parts, at=at):
                part = depth // parts
                for i in range(parts):
                    for b in range(3):
                        place = weights.at[i * part : (i + 1) * part, places[c][b]]
                        pltpu.make_async_copy(pieces[at + i].at[b], place, sems.at[c, b]).start()

            at += parts
    left = jnp.concatenate([g[...] for g in grads], axis=1)
    for c in range(chunks):
        for b in range(3):
            place = weights.at[:, places[c][b]]
            pltpu.make_async_copy(place, place, sems.at[c, b]).wait()
    total = lax.dot_general(left, weights[...], (((1,), (1,)), ((), ())), preferred_element_type=jnp.float32)
    out_ref[...] = total.astype(jnp.bfloat16)


def input_grad(pick, grads, weights, core):
    rows = grads[0].shape[0]
    depth = weights[0][0][0].shape[1]
    inner = sum(g.shape[1] for g in grads)
    halves = [[len(piece) for piece in pieces] for pieces in weights]
    flat = [part for pieces in weights for piece in pieces for part in piece]
    return pl.pallas_call(
        functools.partial(input_grad_kernel, halves, core),
        grid_spec=pltpu.PrefetchScalarGridSpec(
            num_scalar_prefetch=1,
            grid=(1,),
            in_specs=[at_rest(g.shape) for g in grads] + [away()] * len(flat),
            out_specs=at_rest((rows, depth)),
            scratch_shapes=[
                pltpu.VMEM((depth, inner), jnp.bfloat16),
                pltpu.SemaphoreType.DMA((len(grads), 3)),
            ],
        ),
        out_shape=jax.ShapeDtypeStruct((rows, depth), jnp.bfloat16),
        compiler_params=pltpu.CompilerParams(vmem_limit_bytes=60 * 1024 * 1024),
        cost_estimate=pl.CostEstimate(
            flops=2 * rows * depth * inner, bytes_accessed=2 * (inner * (rows + depth) + rows * depth), transcendentals=0
        ),
        name="input_grad",
    )(pick, *grads, *flat)


def exchange(array, axis, bit):
    count = lax.axis_size(axis)
    return lax.ppermute(array, axis, [(i, i ^ bit) for i in range(count)])


def after(value, *others):
    return lax.optimization_barrier((value, *others))[0]


class Plane:
    def __init__(self, blocks):
        self.blocks = blocks
        self.held = [{} for _ in blocks]

    def own(self, c, *gate):
        mine = after(self.blocks[c], *gate) if gate else self.blocks[c]
        self.held[c][2] = [(exchange(mine, "seq", 2),)]
        self.held[c][4] = [(exchange(mine, "seq", 4),)]
        self.held[c][0] = [(mine, exchange(mine, "seq", 1))]

    def came(self, c, *places):
        return [part[0] for where in places for part in self.held[c][where]]

    def swapped(self, c, *places):
        return [part[1] for where in places for part in self.held[c][where]]

    def relay(self, c, *gate):
        far_x, far_y = self.came(c, 2, 4)
        axis = far_x.ndim - 2
        half = far_x.shape[axis] // 2
        low = lax.slice_in_dim(far_x, 0, half, axis=axis)
        high = lax.slice_in_dim(far_y, half, 2 * half, axis=axis)
        if gate:
            low, high = after((low, high), *gate)
        self.held[c][6] = [(exchange(low, "seq", 4),), (exchange(high, "seq", 2),)]

    def swap(self, c, places, *gate):
        for where in places:
            blocks = self.came(c, where)
            if gate:
                blocks = after(blocks, *gate)
            self.held[c][where] = [(part[0], exchange(block, "seq", 1)) for part, block in zip(self.held[c][where], blocks)]

    def pieces(self, c, places=(0, 2, 4, 6)):
        return [[pair[core] for pair in self.held[c][where]] for where in places for core in (0, 1)]


def gather_whole(mine):
    whole = lax.all_gather(mine, "seq", axis=1, tiled=True)
    return [[piece] for piece in jnp.split(whole, BLOCKS, axis=1)]


def local(tokens, proj_weight, residues, decay_rates, skip_gain, grad_out):
    rows = tokens.shape[0]
    depth = proj_weight.shape[0]
    channels = skip_gain.shape[0]
    groups = lax.axis_size("chan")
    me = lax.axis_index("seq").astype(jnp.int32)
    z = lax.axis_index("chan").astype(jnp.int32)
    direct = lax.axis_size("seq") == BLOCKS and groups == 4
    order = jnp.arange(BLOCKS, dtype=jnp.int32)
    if direct:
        order = order ^ me
    coef = coefficients(residues, decay_rates, rows)
    skip = skip_gain[None, :]
    branches = proj_weight.swapaxes(0, 1)
    slots, first = [], 0
    while first < channels:
        width = WIDTHS[min(len(slots), len(WIDTHS) - 1)]
        slots.append(slice(first, first + width))
        first += width
    chunks = len(slots)
    mine = [branches[:, :, lanes] for lanes in slots]

    def forward(c, pieces, part):
        lanes = slots[c]
        count = len(pieces)
        return project(order[BLOCKS - count :], tokens, pieces, part, grad_out[:, lanes], coef[:, :, lanes])

    def meet(made):
        return lax.all_gather(jnp.concatenate([m[2] for m in made], axis=2), "seq")

    def scans(span, made, seen):
        gated, grads = [], []
        start = slots[span[0]].start
        for i, c in enumerate(span):
            lanes = slots[c]
            proj, runs, _ = made[i]
            ends = seen[:, :, :, lanes.start - start : lanes.stop - start]
            gate, grad = scan(me.reshape(1), proj, grad_out[:, lanes], coef[:, :, lanes], skip[:, lanes], runs, ends)
            gated.append(gate)
            grads.append(grad)
        return gated, grads

    if not direct:
        weights = [gather_whole(a) for a in mine]
        made = []
        for c in range(chunks):
            part = project_part(order[:6], tokens, weights[c][:6])
            made.append(forward(c, weights[c][6:], part))
        gated, grads = scans(range(chunks), made, meet(made))
        flat = [jnp.concatenate([p[0][b] for p in pieces], axis=0) for pieces in weights for b in range(3)]
        contract = (((1,), (1,)), ((), ()))
        dx = lax.dot_general(jnp.concatenate(grads, axis=1), jnp.concatenate(flat, axis=1), contract, preferred_element_type=jnp.float32)
        grad_tokens = lax.psum_scatter(dx.astype(jnp.bfloat16), "chan", scatter_dimension=1, tiled=True)
        return (jnp.concatenate(gated, axis=1), grad_tokens)

    plane = Plane(mine)
    near, far = (0, 2, 4), (6,)
    plane.own(0)
    plane.relay(0)
    plane.swap(0, (2, 4))
    plane.own(1, *plane.swapped(0, 0, 2, 4))
    plane.swap(0, far)
    part = project_part(order[:6], tokens, plane.pieces(0, near))
    made = [forward(0, plane.pieces(0, far), part)]
    seen = meet(made)
    plane.relay(1, seen)
    plane.swap(1, (2, 4), seen)
    gated, grads = scans((0,), made, seen)
    part = project_part(order[:6], tokens, plane.pieces(1, near))
    plane.swap(1, far, part, grads[0])
    made.append(forward(1, plane.pieces(1, far), part))
    late = scans((1,), made[1:], meet(made[1:]))
    gated, grads = gated + late[0], grads + late[1]
    weights = [plane.pieces(c) for c in range(chunks)]

    turns = jnp.array([[3, 2, 1, 0], [3, 2, 0, 1], [0, 1, 3, 2], [0, 1, 2, 3]], jnp.int32)[z]
    inwards, across, outwards = [(0, 1), (3, 2)], [(1, 2), (2, 1)], [(1, 0), (2, 3)]

    def part(turn, core):
        pick = me ^ (2 * turns[turn] + core)
        return input_grad(pick.reshape(1), grads, weights, core)

    def add(*terms):
        return sum(t.astype(jnp.float32) for t in terms).astype(jnp.bfloat16)

    sent = []

    def send(block, pairs):
        return lax.ppermute(block, "chan", pairs)

    parts = [[None, None] for _ in range(4)]
    got = [[None, None] for _ in range(3)]
    swapped = [[None, None] for _ in range(3)]
    for turn in range(3):
        for core in range(2):
            parts[turn][core] = part(turn, core)
            block = parts[turn][core]
            if len(sent) >= 2:
                block = after(block, sent[-2])
            got[turn][core] = send(block, inwards)
            sent.append(got[turn][core])
            if turn:
                swapped[turn][core] = send(add(parts[turn - 1][core], got[turn - 1][core]), across)
    out = []
    for core in range(2):
        last = part(3, core)
        back = send(add(parts[2][core], swapped[1][core]), outwards)
        out.append(add(last, got[2][core], swapped[2][core], back))
    return (jnp.concatenate(gated, axis=1), jnp.concatenate(out, axis=1))


def solution(mesh):
    placed = (
        P("seq", None),
        P("seq", None, "chan"),
        P(None, "chan"),
        P(None, "chan"),
        P("chan"),
        P("seq", "chan"),
    )
    return jax.shard_map(
        local,
        mesh=mesh,
        in_specs=placed,
        out_specs=(P("seq", "chan"), P("seq", "chan")),
        check_vma=False,
    )
```

```python
import functools

import jax
import jax.numpy as jnp
from jax import lax
from jax.experimental import pallas as pl
from jax.experimental.pallas import tpu as pltpu
from jax.sharding import PartitionSpec as P

LANES = 128
WIDTHS = (256, 256)
SUBS = 8
MODES = 16
BLOCKS = 8
VMEM_BYTES = 60 * 1024 * 1024


def coefficients(residues, decay_rates, rows):
    return jnp.stack(
        [
            jnp.exp(-decay_rates),
            residues * jnp.sqrt(-jnp.expm1(-2.0 * decay_rates)),
            jnp.exp(-decay_rates * (rows // SUBS)),
            jnp.exp(-decay_rates * rows),
        ]
    )


def spread(coef_ref, which, lanes):
    table = coef_ref[which, :, lanes]
    return [jnp.broadcast_to(table[r : r + 1, :], (SUBS, LANES)) for r in range(MODES)]


def end_states(signal_ref, lanes, decay, run, backward):
    def step(j, state):
        at = run - 1 - j if backward else j
        row = signal_ref[pl.ds(at, SUBS, stride=run), lanes]
        return tuple(a * s + row for a, s in zip(decay, state))

    zero = jnp.zeros((SUBS, LANES), jnp.float32)
    return lax.fori_loop(0, run, step, (zero,) * MODES, unroll=8)


def full_scan(signal_ref, out_ref, decay, gain, state, run, backward):
    def step(j, state):
        at = run - 1 - j if backward else j
        rows = pl.ds(at, SUBS, stride=run)
        row = signal_ref[rows, :]
        state = tuple(a * s + row for a, s in zip(decay, state))
        terms = [g * s for g, s in zip(gain, state)]
        while len(terms) > 1:
            terms = [terms[i] + terms[i + 1] for i in range(0, len(terms), 2)]
        out_ref[rows, :] = terms[0]
        return state

    lax.fori_loop(0, run, step, tuple(state), unroll=8)


def bring(sources, targets, sems):
    copies = [pltpu.make_async_copy(a, b, sems.at[i]) for i, (a, b) in enumerate(zip(sources, targets))]
    for copy in copies:
        copy.start()
    return copies


def product(order_ref, x_ref, pieces, halves, x, w, x_sems, w_sems):
    depth = x.shape[2]
    width = w.shape[2] // 3
    loads, at = [], 0
    for r, parts in enumerate(halves):
        columns = pl.ds(pl.multiple_of(order_ref[r] * depth, depth), depth)
        load = bring([x_ref.at[:, columns]], [x.at[r]], x_sems.at[pl.ds(r, 1)])
        part = depth // parts
        for i in range(parts):
            targets = [w.at[r, pl.ds(i * part, part), pl.ds(b * width, width)] for b in range(3)]
            load += bring([pieces[at].at[b] for b in range(3)], targets, w_sems.at[at])
            at += 1
        loads.append(load)
    total = None
    for r in range(len(halves)):
        for copy in loads[r]:
            copy.wait()
        term = jnp.dot(x[r], w[r], preferred_element_type=jnp.float32)
        total = term if total is None else total + term
    return total


def project_part_kernel(halves, order_ref, x_ref, *refs):
    count = sum(halves)
    pieces, (out_ref, x, w, x_sems, w_sems) = refs[:count], refs[count:]
    out_ref[...] = product(order_ref, x_ref, pieces, halves, x, w, x_sems, w_sems)


def project_kernel(run, halves, order_ref, x_ref, *refs):
    count = sum(halves)
    pieces, refs = refs[:count], refs[count:]
    part_ref, g_ref, coef_ref, proj_ref, runs_ref, ends_ref, x, w, mix, gmix, x_sems, w_sems = refs
    width = g_ref.shape[1]
    total = part_ref[...] + product(order_ref, x_ref, pieces, halves, x, w, x_sems, w_sems)
    for b in range(3):
        proj_ref[b] = total[:, b * width : (b + 1) * width].astype(jnp.bfloat16)
    for lane in range(0, width, LANES):
        lanes = slice(lane, lane + LANES)
        mix[...] = proj_ref[1, :, lanes].astype(jnp.float32) * proj_ref[2, :, lanes].astype(jnp.float32)
        gmix[...] = g_ref[:, lanes].astype(jnp.float32) * proj_ref[0, :, lanes].astype(jnp.float32)
        decay = spread(coef_ref, 0, lanes)
        long = coef_ref[2, :, lanes]
        for way, signal in enumerate((mix, gmix)):
            state = end_states(signal, slice(None), decay, run, way == 1)
            for r in range(MODES):
                runs_ref[way, lane // LANES, pl.ds(r, SUBS, stride=MODES), :] = state[r]
            total = jnp.zeros((MODES, LANES), jnp.float32)
            for i in range(SUBS):
                at = SUBS - 1 - i if way else i
                total = long * total + runs_ref[way, lane // LANES, at * MODES : (at + 1) * MODES, :]
            ends_ref[way, :, lanes] = total


def scan_kernel(run, place_ref, proj_ref, g_ref, coef_ref, skip_ref, runs_ref, ends_ref, gated_ref, gp_ref, mix, out, start):
    me = place_ref[0]
    count = ends_ref.shape[0]
    width = g_ref.shape[1]
    for lane in range(0, width, LANES):
        lanes = slice(lane, lane + LANES)
        decay = spread(coef_ref, 0, lanes)
        gain = spread(coef_ref, 1, lanes)
        long = coef_ref[2, :, lanes]
        whole = coef_ref[3, :, lanes]
        skip = skip_ref[:, lanes]
        grad = g_ref[:, lanes].astype(jnp.float32)
        query, key, value = [proj_ref[b, :, lanes].astype(jnp.float32) for b in range(3)]
        for way in range(2):
            state = jnp.zeros((MODES, LANES), jnp.float32)
            for i in range(count - 1):
                at = count - 1 - i if way else i
                keep = me < at if way else at < me
                state = jnp.where(keep, whole * state + ends_ref[at, way, :, lanes], state)
            for i in range(SUBS):
                at = SUBS - 1 - i if way else i
                start[at * MODES : (at + 1) * MODES, :] = state
                state = long * state + runs_ref[way, lane // LANES, at * MODES : (at + 1) * MODES, :]
            first = [start[pl.ds(r, SUBS, stride=MODES), :] for r in range(MODES)]
            mix[...] = grad * query if way else key * value
            full_scan(mix, out, decay, gain, first, run, way == 1)
            filtered = out[...] + skip * mix[...]
            if way:
                gp_ref[:, width + lane : width + lane + LANES] = (filtered * value).astype(jnp.bfloat16)
                gp_ref[:, 2 * width + lane : 2 * width + lane + LANES] = (filtered * key).astype(jnp.bfloat16)
            else:
                gated_ref[:, lanes] = (query * filtered).astype(jnp.bfloat16)
                gp_ref[:, lane : lane + LANES] = (grad * filtered).astype(jnp.bfloat16)


def at_rest(shape):
    return pl.BlockSpec(shape, lambda *_: (0,) * len(shape))


def away():
    return pl.BlockSpec(memory_space=pltpu.HBM)


def block_scratch(tokens, pieces, width):
    rows, inputs = tokens.shape
    depth = inputs // BLOCKS
    parts = [len(piece) for piece in pieces]
    buffers = [
        pltpu.VMEM((len(pieces), rows, depth), tokens.dtype),
        pltpu.VMEM((len(pieces), depth, 3 * width), tokens.dtype),
    ]
    return parts, buffers, [pltpu.SemaphoreType.DMA((len(pieces),)), pltpu.SemaphoreType.DMA((sum(parts), 3))]


def product_cost(tokens, pieces, width):
    rows = tokens.shape[0]
    depth = tokens.shape[1] // BLOCKS * len(pieces)
    return pl.CostEstimate(
        flops=2 * rows * depth * 3 * width, bytes_accessed=2 * depth * (rows + 3 * width), transcendentals=0
    )


def project_part(order, tokens, pieces):
    rows = tokens.shape[0]
    flat = [part for piece in pieces for part in piece]
    width = flat[0].shape[2]
    halves, buffers, sems = block_scratch(tokens, pieces, width)
    return pl.pallas_call(
        functools.partial(project_part_kernel, halves),
        grid_spec=pltpu.PrefetchScalarGridSpec(
            num_scalar_prefetch=1,
            grid=(1,),
            in_specs=[away()] * (1 + len(flat)),
            out_specs=at_rest((rows, 3 * width)),
            scratch_shapes=buffers + sems,
        ),
        out_shape=jax.ShapeDtypeStruct((rows, 3 * width), jnp.float32),
        compiler_params=pltpu.CompilerParams(vmem_limit_bytes=48 * 1024 * 1024),
        cost_estimate=product_cost(tokens, pieces, width),
        name="project_part",
    )(order, tokens, *flat)


def project(order, tokens, pieces, part, grad_out, coef):
    rows = tokens.shape[0]
    width = grad_out.shape[1]
    flat = [part for piece in pieces for part in piece]
    groups = width // LANES
    halves, buffers, sems = block_scratch(tokens, pieces, width)
    return pl.pallas_call(
        functools.partial(project_kernel, rows // SUBS, halves),
        grid_spec=pltpu.PrefetchScalarGridSpec(
            num_scalar_prefetch=1,
            grid=(1,),
            in_specs=[away()] * (1 + len(flat)) + [at_rest(a.shape) for a in (part, grad_out, coef)],
            out_specs=[
                at_rest((3, rows, width)),
                at_rest((2, groups, SUBS * MODES, LANES)),
                at_rest((2, MODES, width)),
            ],
            scratch_shapes=buffers
            + [
                pltpu.VMEM((rows, LANES), jnp.float32),
                pltpu.VMEM((rows, LANES), jnp.float32),
            ]
            + sems,
        ),
        out_shape=[
            jax.ShapeDtypeStruct((3, rows, width), jnp.bfloat16),
            jax.ShapeDtypeStruct((2, groups, SUBS * MODES, LANES), jnp.float32),
            jax.ShapeDtypeStruct((2, MODES, width), jnp.float32),
        ],
        compiler_params=pltpu.CompilerParams(vmem_limit_bytes=48 * 1024 * 1024),
        cost_estimate=product_cost(tokens, pieces, width),
        name="project",
    )(order, tokens, *flat, part, grad_out, coef)


def scan(place, proj, grad_out, coef, skip, runs, ends):
    _, rows, width = proj.shape
    return pl.pallas_call(
        functools.partial(scan_kernel, rows // SUBS),
        grid_spec=pltpu.PrefetchScalarGridSpec(
            num_scalar_prefetch=1,
            grid=(1,),
            in_specs=[at_rest(a.shape) for a in (proj, grad_out, coef, skip, runs, ends)],
            out_specs=[at_rest((rows, width)), at_rest((rows, 3 * width))],
            scratch_shapes=[
                pltpu.VMEM((rows, LANES), jnp.float32),
                pltpu.VMEM((rows, LANES), jnp.float32),
                pltpu.VMEM((SUBS * MODES, LANES), jnp.float32),
            ],
        ),
        out_shape=[
            jax.ShapeDtypeStruct((rows, width), jnp.bfloat16),
            jax.ShapeDtypeStruct((rows, 3 * width), jnp.bfloat16),
        ],
        compiler_params=pltpu.CompilerParams(vmem_limit_bytes=VMEM_BYTES // 4),
        cost_estimate=pl.CostEstimate(flops=rows * width * MODES * 16, bytes_accessed=12 * rows * width, transcendentals=0),
        name="scan",
    )(place, proj, grad_out, coef, skip, runs, ends)


def input_grad_kernel(halves, core, pick_ref, *refs):
    chunks = len(halves)
    counts = [sum(h) for h in halves]
    places, total = [], 0
    for c in range(chunks):
        width = refs[c].shape[1] // 3
        places.append([slice(total + b * width, total + (b + 1) * width) for b in range(3)])
        total += 3 * width
    grads, refs = refs[:chunks], refs[chunks:]
    pieces, refs = refs[: sum(counts)], refs[sum(counts) :]
    out_ref, weights, sems = refs
    r_wanted = pick_ref[0]
    depth = weights.shape[0]
    at = 0
    for c, parts_of in enumerate(halves):
        for r, parts in enumerate(parts_of):

            @pl.when(r_wanted == r)
            def _(c=c, r=r, parts=parts, at=at):
                part = depth // parts
                for i in range(parts):
                    for b in range(3):
                        place = weights.at[i * part : (i + 1) * part, places[c][b]]
                        pltpu.make_async_copy(pieces[at + i].at[b], place, sems.at[c, b]).start()

            at += parts
    left = jnp.concatenate([g[...] for g in grads], axis=1)
    for c in range(chunks):
        for b in range(3):
            place = weights.at[:, places[c][b]]
            pltpu.make_async_copy(place, place, sems.at[c, b]).wait()
    tile = depth // 2

    @pl.loop(0, depth // tile)
    def _(i):
        here = pl.ds(pl.multiple_of(i * tile, tile), tile)
        total = lax.dot_general(left, weights[here, :], (((1,), (1,)), ((), ())), preferred_element_type=jnp.float32)
        out_ref[:, here] = total.astype(jnp.bfloat16)


def input_grad(pick, grads, weights, core):
    rows = grads[0].shape[0]
    depth = weights[0][0][0].shape[1]
    inner = sum(g.shape[1] for g in grads)
    halves = [[len(piece) for piece in pieces] for pieces in weights]
    flat = [part for pieces in weights for piece in pieces for part in piece]
    return pl.pallas_call(
        functools.partial(input_grad_kernel, halves, core),
        grid_spec=pltpu.PrefetchScalarGridSpec(
            num_scalar_prefetch=1,
            grid=(1,),
            in_specs=[at_rest(g.shape) for g in grads] + [away()] * len(flat),
            out_specs=at_rest((rows, depth)),
            scratch_shapes=[
                pltpu.VMEM((depth, inner), jnp.bfloat16),
                pltpu.SemaphoreType.DMA((len(grads), 3)),
            ],
        ),
        out_shape=jax.ShapeDtypeStruct((rows, depth), jnp.bfloat16),
        compiler_params=pltpu.CompilerParams(vmem_limit_bytes=60 * 1024 * 1024),
        cost_estimate=pl.CostEstimate(
            flops=2 * rows * depth * inner, bytes_accessed=2 * (inner * (rows + depth) + rows * depth), transcendentals=0
        ),
        name="input_grad",
    )(pick, *grads, *flat)


def exchange(array, axis, bit):
    count = lax.axis_size(axis)
    return lax.ppermute(array, axis, [(i, i ^ bit) for i in range(count)])


def after(value, *others):
    return lax.optimization_barrier((value, *others))[0]


class Plane:
    def __init__(self, blocks):
        self.blocks = blocks
        self.held = [{} for _ in blocks]

    def own(self, c, *gate):
        mine = after(self.blocks[c], *gate) if gate else self.blocks[c]
        self.held[c][2] = [(exchange(mine, "seq", 2),)]
        self.held[c][4] = [(exchange(mine, "seq", 4),)]
        self.held[c][0] = [(mine, exchange(mine, "seq", 1))]

    def came(self, c, *places):
        return [part[0] for where in places for part in self.held[c][where]]

    def swapped(self, c, *places):
        return [part[1] for where in places for part in self.held[c][where]]

    def relay(self, c, *gate):
        far_x, far_y = self.came(c, 2, 4)
        axis = far_x.ndim - 2
        half = far_x.shape[axis] // 2
        low = lax.slice_in_dim(far_x, 0, half, axis=axis)
        high = lax.slice_in_dim(far_y, half, 2 * half, axis=axis)
        if gate:
            low, high = after((low, high), *gate)
        self.held[c][6] = [(exchange(low, "seq", 4),), (exchange(high, "seq", 2),)]

    def swap(self, c, places, *gate):
        for where in places:
            blocks = self.came(c, where)
            if gate:
                blocks = after(blocks, *gate)
            self.held[c][where] = [(part[0], exchange(block, "seq", 1)) for part, block in zip(self.held[c][where], blocks)]

    def pieces(self, c, places=(0, 2, 4, 6)):
        return [[pair[core] for pair in self.held[c][where]] for where in places for core in (0, 1)]


def gather_whole(mine):
    whole = lax.all_gather(mine, "seq", axis=1, tiled=True)
    return [[piece] for piece in jnp.split(whole, BLOCKS, axis=1)]


def local(tokens, proj_weight, residues, decay_rates, skip_gain, grad_out):
    rows = tokens.shape[0]
    depth = proj_weight.shape[0]
    channels = skip_gain.shape[0]
    groups = lax.axis_size("chan")
    me = lax.axis_index("seq").astype(jnp.int32)
    z = lax.axis_index("chan").astype(jnp.int32)
    direct = lax.axis_size("seq") == BLOCKS and groups == 4
    order = jnp.arange(BLOCKS, dtype=jnp.int32)
    if direct:
        order = order ^ me
    coef = coefficients(residues, decay_rates, rows)
    skip = skip_gain[None, :]
    branches = proj_weight.swapaxes(0, 1)
    slots, first = [], 0
    while first < channels:
        width = WIDTHS[min(len(slots), len(WIDTHS) - 1)]
        slots.append(slice(first, first + width))
        first += width
    chunks = len(slots)
    mine = [branches[:, :, lanes] for lanes in slots]

    def forward(c, pieces, part):
        lanes = slots[c]
        count = len(pieces)
        return project(order[BLOCKS - count :], tokens, pieces, part, grad_out[:, lanes], coef[:, :, lanes])

    def meet(made):
        return lax.all_gather(jnp.concatenate([m[2] for m in made], axis=2), "seq")

    def scans(span, made, seen):
        gated, grads = [], []
        start = slots[span[0]].start
        for i, c in enumerate(span):
            lanes = slots[c]
            proj, runs, _ = made[i]
            ends = seen[:, :, :, lanes.start - start : lanes.stop - start]
            gate, grad = scan(me.reshape(1), proj, grad_out[:, lanes], coef[:, :, lanes], skip[:, lanes], runs, ends)
            gated.append(gate)
            grads.append(grad)
        return gated, grads

    if not direct:
        weights = [gather_whole(a) for a in mine]
        made = []
        for c in range(chunks):
            part = project_part(order[:6], tokens, weights[c][:6])
            made.append(forward(c, weights[c][6:], part))
        gated, grads = scans(range(chunks), made, meet(made))
        flat = [jnp.concatenate([p[0][b] for p in pieces], axis=0) for pieces in weights for b in range(3)]
        contract = (((1,), (1,)), ((), ()))
        dx = lax.dot_general(jnp.concatenate(grads, axis=1), jnp.concatenate(flat, axis=1), contract, preferred_element_type=jnp.float32)
        grad_tokens = lax.psum_scatter(dx.astype(jnp.bfloat16), "chan", scatter_dimension=1, tiled=True)
        return (jnp.concatenate(gated, axis=1), grad_tokens)

    plane = Plane(mine)
    near, far = (0, 2, 4), (6,)
    plane.own(0)
    plane.relay(0)
    plane.swap(0, (2, 4))
    plane.own(1, *plane.swapped(0, 0, 2, 4))
    plane.swap(0, far)
    part = project_part(order[:6], tokens, plane.pieces(0, near))
    made = [forward(0, plane.pieces(0, far), part)]
    seen = meet(made)
    plane.relay(1, seen)
    plane.swap(1, (2, 4), seen)
    gated, grads = scans((0,), made, seen)
    part = project_part(order[:6], tokens, plane.pieces(1, near))
    plane.swap(1, far, part, grads[0])
    made.append(forward(1, plane.pieces(1, far), part))
    late = scans((1,), made[1:], meet(made[1:]))
    gated, grads = gated + late[0], grads + late[1]
    weights = [plane.pieces(c) for c in range(chunks)]

    turns = jnp.array([[3, 2, 1, 0], [3, 2, 0, 1], [0, 1, 3, 2], [0, 1, 2, 3]], jnp.int32)[z]
    inwards, across, outwards = [(0, 1), (3, 2)], [(1, 2), (2, 1)], [(1, 0), (2, 3)]

    def part(turn, core):
        pick = me ^ (2 * turns[turn] + core)
        return input_grad(pick.reshape(1), grads, weights, core)

    def add(*terms):
        return sum(t.astype(jnp.float32) for t in terms).astype(jnp.bfloat16)

    sent = []

    def send(block, pairs):
        return lax.ppermute(block, "chan", pairs)

    parts = [[None, None] for _ in range(4)]
    got = [[None, None] for _ in range(3)]
    swapped = [[None, None] for _ in range(3)]
    for turn in range(3):
        for core in range(2):
            parts[turn][core] = part(turn, core)
            block = parts[turn][core]
            if len(sent) >= 2:
                block = after(block, sent[-2])
            got[turn][core] = send(block, inwards)
            sent.append(got[turn][core])
            if turn:
                swapped[turn][core] = send(add(parts[turn - 1][core], got[turn - 1][core]), across)
    out = []
    for core in range(2):
        last = part(3, core)
        back = send(add(parts[2][core], swapped[1][core]), outwards)
        out.append(add(last, got[2][core], swapped[2][core], back))
    return (jnp.concatenate(gated, axis=1), jnp.concatenate(out, axis=1))


def solution(mesh):
    placed = (
        P("seq", None),
        P("seq", None, "chan"),
        P(None, "chan"),
        P(None, "chan"),
        P("chan"),
        P("seq", "chan"),
    )
    return jax.shard_map(
        local,
        mesh=mesh,
        in_specs=placed,
        out_specs=(P("seq", "chan"), P("seq", "chan")),
        check_vma=False,
    )
```

```python
import functools

import jax
import jax.numpy as jnp
from jax import lax
from jax.experimental import pallas as pl
from jax.experimental.pallas import tpu as pltpu
from jax.sharding import PartitionSpec as P

LANES = 128
WIDTHS = (256, 256)
SUBS = 8
MODES = 16
BLOCKS = 8
VMEM_BYTES = 60 * 1024 * 1024


def coefficients(residues, decay_rates, rows):
    return jnp.stack(
        [
            jnp.exp(-decay_rates),
            residues * jnp.sqrt(-jnp.expm1(-2.0 * decay_rates)),
            jnp.exp(-decay_rates * (rows // SUBS)),
            jnp.exp(-decay_rates * rows),
        ]
    )


def spread(coef_ref, which, lanes):
    table = coef_ref[which, :, lanes]
    return [jnp.broadcast_to(table[r : r + 1, :], (SUBS, LANES)) for r in range(MODES)]


def end_states(signal_ref, lanes, decay, run, backward):
    def step(j, state):
        at = run - 1 - j if backward else j
        row = signal_ref[pl.ds(at, SUBS, stride=run), lanes]
        return tuple(a * s + row for a, s in zip(decay, state))

    zero = jnp.zeros((SUBS, LANES), jnp.float32)
    return lax.fori_loop(0, run, step, (zero,) * MODES, unroll=8)


def full_scan(signal_ref, out_ref, decay, gain, state, run, backward):
    def step(j, state):
        at = run - 1 - j if backward else j
        rows = pl.ds(at, SUBS, stride=run)
        row = signal_ref[rows, :]
        state = tuple(a * s + row for a, s in zip(decay, state))
        terms = [g * s for g, s in zip(gain, state)]
        while len(terms) > 1:
            terms = [terms[i] + terms[i + 1] for i in range(0, len(terms), 2)]
        out_ref[rows, :] = terms[0]
        return state

    lax.fori_loop(0, run, step, tuple(state), unroll=8)


def bring(sources, targets, sems):
    copies = [pltpu.make_async_copy(a, b, sems.at[i]) for i, (a, b) in enumerate(zip(sources, targets))]
    for copy in copies:
        copy.start()
    return copies


def product(order_ref, x_ref, pieces, halves, x, w, x_sems, w_sems):
    depth = x.shape[2]
    width = w.shape[2] // 3
    loads, at = [], 0
    for r, parts in enumerate(halves):
        columns = pl.ds(pl.multiple_of(order_ref[r] * depth, depth), depth)
        load = bring([x_ref.at[:, columns]], [x.at[r]], x_sems.at[pl.ds(r, 1)])
        part = depth // parts
        for i in range(parts):
            targets = [w.at[r, pl.ds(i * part, part), pl.ds(b * width, width)] for b in range(3)]
            load += bring([pieces[at].at[b] for b in range(3)], targets, w_sems.at[at])
            at += 1
        loads.append(load)
    total = None
    for r in range(len(halves)):
        for copy in loads[r]:
            copy.wait()
        term = jnp.dot(x[r], w[r], preferred_element_type=jnp.float32)
        total = term if total is None else total + term
    return total


def project_part_kernel(halves, order_ref, x_ref, *refs):
    count = sum(halves)
    pieces, (out_ref, x, w, x_sems, w_sems) = refs[:count], refs[count:]
    out_ref[...] = product(order_ref, x_ref, pieces, halves, x, w, x_sems, w_sems)


def project_kernel(run, halves, order_ref, x_ref, *refs):
    count = sum(halves)
    pieces, refs = refs[:count], refs[count:]
    part_ref, g_ref, coef_ref, proj_ref, runs_ref, ends_ref, x, w, mix, gmix, x_sems, w_sems = refs
    width = g_ref.shape[1]
    total = part_ref[...] + product(order_ref, x_ref, pieces, halves, x, w, x_sems, w_sems)
    for b in range(3):
        proj_ref[b] = total[:, b * width : (b + 1) * width].astype(jnp.bfloat16)
    for lane in range(0, width, LANES):
        lanes = slice(lane, lane + LANES)
        mix[...] = proj_ref[1, :, lanes].astype(jnp.float32) * proj_ref[2, :, lanes].astype(jnp.float32)
        gmix[...] = g_ref[:, lanes].astype(jnp.float32) * proj_ref[0, :, lanes].astype(jnp.float32)
        decay = spread(coef_ref, 0, lanes)
        long = coef_ref[2, :, lanes]
        for way, signal in enumerate((mix, gmix)):
            state = end_states(signal, slice(None), decay, run, way == 1)
            for r in range(MODES):
                runs_ref[way, lane // LANES, pl.ds(r, SUBS, stride=MODES), :] = state[r]
            total = jnp.zeros((MODES, LANES), jnp.float32)
            for i in range(SUBS):
                at = SUBS - 1 - i if way else i
                total = long * total + runs_ref[way, lane // LANES, at * MODES : (at + 1) * MODES, :]
            ends_ref[way, :, lanes] = total


def scan_kernel(run, place_ref, proj_ref, g_ref, coef_ref, skip_ref, runs_ref, ends_ref, gated_ref, gp_ref, mix, out, start):
    me = place_ref[0]
    count = ends_ref.shape[0]
    width = g_ref.shape[1]
    for lane in range(0, width, LANES):
        lanes = slice(lane, lane + LANES)
        decay = spread(coef_ref, 0, lanes)
        gain = spread(coef_ref, 1, lanes)
        long = coef_ref[2, :, lanes]
        whole = coef_ref[3, :, lanes]
        skip = skip_ref[:, lanes]
        grad = g_ref[:, lanes].astype(jnp.float32)
        query, key, value = [proj_ref[b, :, lanes].astype(jnp.float32) for b in range(3)]
        for way in range(2):
            state = jnp.zeros((MODES, LANES), jnp.float32)
            for i in range(count - 1):
                at = count - 1 - i if way else i
                keep = me < at if way else at < me
                state = jnp.where(keep, whole * state + ends_ref[at, way, :, lanes], state)
            for i in range(SUBS):
                at = SUBS - 1 - i if way else i
                start[at * MODES : (at + 1) * MODES, :] = state
                state = long * state + runs_ref[way, lane // LANES, at * MODES : (at + 1) * MODES, :]
            first = [start[pl.ds(r, SUBS, stride=MODES), :] for r in range(MODES)]
            mix[...] = grad * query if way else key * value
            full_scan(mix, out, decay, gain, first, run, way == 1)
            filtered = out[...] + skip * mix[...]
            if way:
                gp_ref[:, width + lane : width + lane + LANES] = (filtered * value).astype(jnp.bfloat16)
                gp_ref[:, 2 * width + lane : 2 * width + lane + LANES] = (filtered * key).astype(jnp.bfloat16)
            else:
                gated_ref[:, lanes] = (query * filtered).astype(jnp.bfloat16)
                gp_ref[:, lane : lane + LANES] = (grad * filtered).astype(jnp.bfloat16)


def at_rest(shape):
    return pl.BlockSpec(shape, lambda *_: (0,) * len(shape))


def away():
    return pl.BlockSpec(memory_space=pltpu.HBM)


def block_scratch(tokens, pieces, width):
    rows, inputs = tokens.shape
    depth = inputs // BLOCKS
    parts = [len(piece) for piece in pieces]
    buffers = [
        pltpu.VMEM((len(pieces), rows, depth), tokens.dtype),
        pltpu.VMEM((len(pieces), depth, 3 * width), tokens.dtype),
    ]
    return parts, buffers, [pltpu.SemaphoreType.DMA((len(pieces),)), pltpu.SemaphoreType.DMA((sum(parts), 3))]


def product_cost(tokens, pieces, width):
    rows = tokens.shape[0]
    depth = tokens.shape[1] // BLOCKS * len(pieces)
    return pl.CostEstimate(
        flops=2 * rows * depth * 3 * width, bytes_accessed=2 * depth * (rows + 3 * width), transcendentals=0
    )


def project_part(order, tokens, pieces):
    rows = tokens.shape[0]
    flat = [part for piece in pieces for part in piece]
    width = flat[0].shape[2]
    halves, buffers, sems = block_scratch(tokens, pieces, width)
    return pl.pallas_call(
        functools.partial(project_part_kernel, halves),
        grid_spec=pltpu.PrefetchScalarGridSpec(
            num_scalar_prefetch=1,
            grid=(1,),
            in_specs=[away()] * (1 + len(flat)),
            out_specs=at_rest((rows, 3 * width)),
            scratch_shapes=buffers + sems,
        ),
        out_shape=jax.ShapeDtypeStruct((rows, 3 * width), jnp.float32),
        compiler_params=pltpu.CompilerParams(vmem_limit_bytes=48 * 1024 * 1024),
        cost_estimate=product_cost(tokens, pieces, width),
        name="project_part",
    )(order, tokens, *flat)


def project(order, tokens, pieces, part, grad_out, coef):
    rows = tokens.shape[0]
    width = grad_out.shape[1]
    flat = [part for piece in pieces for part in piece]
    groups = width // LANES
    halves, buffers, sems = block_scratch(tokens, pieces, width)
    return pl.pallas_call(
        functools.partial(project_kernel, rows // SUBS, halves),
        grid_spec=pltpu.PrefetchScalarGridSpec(
            num_scalar_prefetch=1,
            grid=(1,),
            in_specs=[away()] * (1 + len(flat)) + [at_rest(a.shape) for a in (part, grad_out, coef)],
            out_specs=[
                at_rest((3, rows, width)),
                at_rest((2, groups, SUBS * MODES, LANES)),
                at_rest((2, MODES, width)),
            ],
            scratch_shapes=buffers
            + [
                pltpu.VMEM((rows, LANES), jnp.float32),
                pltpu.VMEM((rows, LANES), jnp.float32),
            ]
            + sems,
        ),
        out_shape=[
            jax.ShapeDtypeStruct((3, rows, width), jnp.bfloat16),
            jax.ShapeDtypeStruct((2, groups, SUBS * MODES, LANES), jnp.float32),
            jax.ShapeDtypeStruct((2, MODES, width), jnp.float32),
        ],
        compiler_params=pltpu.CompilerParams(vmem_limit_bytes=48 * 1024 * 1024),
        cost_estimate=product_cost(tokens, pieces, width),
        name="project",
    )(order, tokens, *flat, part, grad_out, coef)


def scan(place, proj, grad_out, coef, skip, runs, ends):
    _, rows, width = proj.shape
    return pl.pallas_call(
        functools.partial(scan_kernel, rows // SUBS),
        grid_spec=pltpu.PrefetchScalarGridSpec(
            num_scalar_prefetch=1,
            grid=(1,),
            in_specs=[at_rest(a.shape) for a in (proj, grad_out, coef, skip, runs, ends)],
            out_specs=[at_rest((rows, width)), at_rest((rows, 3 * width))],
            scratch_shapes=[
                pltpu.VMEM((rows, LANES), jnp.float32),
                pltpu.VMEM((rows, LANES), jnp.float32),
                pltpu.VMEM((SUBS * MODES, LANES), jnp.float32),
            ],
        ),
        out_shape=[
            jax.ShapeDtypeStruct((rows, width), jnp.bfloat16),
            jax.ShapeDtypeStruct((rows, 3 * width), jnp.bfloat16),
        ],
        compiler_params=pltpu.CompilerParams(vmem_limit_bytes=48 * 1024 * 1024),
        cost_estimate=pl.CostEstimate(flops=rows * width * MODES * 16, bytes_accessed=12 * rows * width, transcendentals=0),
        name="scan",
    )(place, proj, grad_out, coef, skip, runs, ends)


def input_grad_kernel(halves, half, pick_ref, *refs):
    chunks = len(halves)
    counts = [sum(h) for h in halves]
    places, total = [], 0
    for c in range(chunks):
        width = refs[c].shape[1] // 3
        places.append([slice(total + b * width, total + (b + 1) * width) for b in range(3)])
        total += 3 * width
    grads, refs = refs[:chunks], refs[chunks:]
    pieces, refs = refs[: sum(counts)], refs[sum(counts) :]
    out_ref, weights, sems = refs
    r_wanted = pick_ref[0]
    depth = weights.shape[0]
    at = 0
    for c, parts_of in enumerate(halves):
        for r, parts in enumerate(parts_of):

            @pl.when(r_wanted == r)
            def _(c=c, r=r, parts=parts, at=at):
                if half is None:
                    part = depth // parts
                    moves = [(pieces[at + i], slice(i * part, (i + 1) * part)) for i in range(parts)]
                elif parts == 2:
                    moves = [(pieces[at + half], slice(0, depth))]
                else:
                    moves = [(pieces[at].at[:, half * depth : (half + 1) * depth, :], slice(0, depth))]
                for source, rows in moves:
                    for b in range(3):
                        pltpu.make_async_copy(source.at[b], weights.at[rows, places[c][b]], sems.at[c, b]).start()

            at += parts
    left = jnp.concatenate([g[...] for g in grads], axis=1)
    for c in range(chunks):
        for b in range(3):
            place = weights.at[:, places[c][b]]
            pltpu.make_async_copy(place, place, sems.at[c, b]).wait()
    tile = depth // 2

    @pl.loop(0, depth // tile)
    def _(i):
        here = pl.ds(pl.multiple_of(i * tile, tile), tile)
        total = lax.dot_general(left, weights[here, :], (((1,), (1,)), ((), ())), preferred_element_type=jnp.float32)
        out_ref[:, here] = total.astype(jnp.bfloat16)


def input_grad(pick, grads, weights, half=None):
    rows = grads[0].shape[0]
    depth = weights[0][0][0].shape[1] // (1 if half is None else 2)
    inner = sum(g.shape[1] for g in grads)
    halves = [[len(piece) for piece in pieces] for pieces in weights]
    flat = [part for pieces in weights for piece in pieces for part in piece]
    return pl.pallas_call(
        functools.partial(input_grad_kernel, halves, half),
        grid_spec=pltpu.PrefetchScalarGridSpec(
            num_scalar_prefetch=1,
            grid=(1,),
            in_specs=[at_rest(g.shape) for g in grads] + [away()] * len(flat),
            out_specs=at_rest((rows, depth)),
            scratch_shapes=[
                pltpu.VMEM((depth, inner), jnp.bfloat16),
                pltpu.SemaphoreType.DMA((len(grads), 3)),
            ],
        ),
        out_shape=jax.ShapeDtypeStruct((rows, depth), jnp.bfloat16),
        compiler_params=pltpu.CompilerParams(vmem_limit_bytes=(60 if half is None else 32) * 1024 * 1024),
        cost_estimate=pl.CostEstimate(
            flops=2 * rows * depth * inner, bytes_accessed=2 * (inner * (rows + depth) + rows * depth), transcendentals=0
        ),
        name="input_grad",
    )(pick, *grads, *flat)


def exchange(array, axis, bit):
    count = lax.axis_size(axis)
    return lax.ppermute(array, axis, [(i, i ^ bit) for i in range(count)])


def after(value, *others):
    return lax.optimization_barrier((value, *others))[0]


class Plane:
    def __init__(self, blocks):
        self.blocks = blocks
        self.held = [{} for _ in blocks]

    def own(self, c, *gate):
        mine = after(self.blocks[c], *gate) if gate else self.blocks[c]
        self.held[c][2] = [(exchange(mine, "seq", 2),)]
        self.held[c][4] = [(exchange(mine, "seq", 4),)]
        self.held[c][0] = [(mine, exchange(mine, "seq", 1))]

    def came(self, c, *places):
        return [part[0] for where in places for part in self.held[c][where]]

    def swapped(self, c, *places):
        return [part[1] for where in places for part in self.held[c][where]]

    def relay(self, c, *gate):
        far_x, far_y = self.came(c, 2, 4)
        axis = far_x.ndim - 2
        half = far_x.shape[axis] // 2
        low = lax.slice_in_dim(far_x, 0, half, axis=axis)
        high = lax.slice_in_dim(far_y, half, 2 * half, axis=axis)
        if gate:
            low, high = after((low, high), *gate)
        self.held[c][6] = [(exchange(low, "seq", 4),), (exchange(high, "seq", 2),)]

    def swap(self, c, places, *gate):
        for where in places:
            blocks = self.came(c, where)
            if gate:
                blocks = after(blocks, *gate)
            self.held[c][where] = [(part[0], exchange(block, "seq", 1)) for part, block in zip(self.held[c][where], blocks)]

    def pieces(self, c, places=(0, 2, 4, 6)):
        return [[pair[core] for pair in self.held[c][where]] for where in places for core in (0, 1)]


def gather_whole(mine):
    whole = lax.all_gather(mine, "seq", axis=1, tiled=True)
    return [[piece] for piece in jnp.split(whole, BLOCKS, axis=1)]


def local(tokens, proj_weight, residues, decay_rates, skip_gain, grad_out):
    rows = tokens.shape[0]
    depth = proj_weight.shape[0]
    channels = skip_gain.shape[0]
    groups = lax.axis_size("chan")
    me = lax.axis_index("seq").astype(jnp.int32)
    z = lax.axis_index("chan").astype(jnp.int32)
    direct = lax.axis_size("seq") == BLOCKS and groups == 4
    order = jnp.arange(BLOCKS, dtype=jnp.int32)
    if direct:
        order = order ^ me
    coef = coefficients(residues, decay_rates, rows)
    skip = skip_gain[None, :]
    branches = proj_weight.swapaxes(0, 1)
    slots, first = [], 0
    while first < channels:
        width = WIDTHS[min(len(slots), len(WIDTHS) - 1)]
        slots.append(slice(first, first + width))
        first += width
    chunks = len(slots)
    mine = [branches[:, :, lanes] for lanes in slots]

    def forward(c, pieces, part):
        lanes = slots[c]
        count = len(pieces)
        return project(order[BLOCKS - count :], tokens, pieces, part, grad_out[:, lanes], coef[:, :, lanes])

    def meet(made):
        return lax.all_gather(jnp.concatenate([m[2] for m in made], axis=2), "seq")

    def scans(span, made, seen):
        gated, grads = [], []
        start = slots[span[0]].start
        for i, c in enumerate(span):
            lanes = slots[c]
            proj, runs, _ = made[i]
            ends = seen[:, :, :, lanes.start - start : lanes.stop - start]
            gate, grad = scan(me.reshape(1), proj, grad_out[:, lanes], coef[:, :, lanes], skip[:, lanes], runs, ends)
            gated.append(gate)
            grads.append(grad)
        return gated, grads

    if not direct:
        weights = [gather_whole(a) for a in mine]
        made = []
        for c in range(chunks):
            part = project_part(order[:6], tokens, weights[c][:6])
            made.append(forward(c, weights[c][6:], part))
        gated, grads = scans(range(chunks), made, meet(made))
        flat = [jnp.concatenate([p[0][b] for p in pieces], axis=0) for pieces in weights for b in range(3)]
        contract = (((1,), (1,)), ((), ()))
        dx = lax.dot_general(jnp.concatenate(grads, axis=1), jnp.concatenate(flat, axis=1), contract, preferred_element_type=jnp.float32)
        grad_tokens = lax.psum_scatter(dx.astype(jnp.bfloat16), "chan", scatter_dimension=1, tiled=True)
        return (jnp.concatenate(gated, axis=1), grad_tokens)

    plane = Plane(mine)
    near, far = (0, 2, 4), (6,)
    plane.own(0)
    plane.relay(0)
    plane.swap(0, (2, 4))
    plane.own(1, *plane.swapped(0, 0, 2, 4))
    plane.swap(0, far)
    part = project_part(order[:6], tokens, plane.pieces(0, near))
    made = [forward(0, plane.pieces(0, far), part)]
    seen = meet(made)
    plane.relay(1, seen)
    plane.swap(1, (2, 4), seen)
    gated, grads = scans((0,), made, seen)
    part = project_part(order[:6], tokens, plane.pieces(1, near))
    plane.swap(1, far, part, grads[0])
    made.append(forward(1, plane.pieces(1, far), part))
    late = scans((1,), made[1:], meet(made[1:]))
    gated, grads = gated + late[0], grads + late[1]
    weights = [plane.pieces(c) for c in range(chunks)]

    turns = jnp.array([[3, 2, 1, 0], [3, 2, 0, 1], [0, 1, 3, 2], [0, 1, 2, 3]], jnp.int32)[z]
    inwards, across, outwards = [(0, 1), (3, 2)], [(1, 2), (2, 1)], [(1, 0), (2, 3)]

    def part(turn, core, half=None):
        pick = me ^ (2 * turns[turn] + core)
        return input_grad(pick.reshape(1), grads, weights, half)

    def add(*terms):
        return sum(t.astype(jnp.float32) for t in terms).astype(jnp.bfloat16)

    sent = []

    def send(block, pairs):
        return lax.ppermute(block, "chan", pairs)

    parts = [[None, None] for _ in range(4)]
    got = [[None, None] for _ in range(3)]
    swapped = [[None, None] for _ in range(3)]
    for turn in range(3):
        for core in range(2):
            if turn == core == 0:
                pair = [part(0, 0, half) for half in range(2)]
                parts[0][0] = jnp.concatenate(pair, axis=1)
                got[0][0] = jnp.concatenate([send(block, inwards) for block in pair], axis=1)
                sent.append(got[0][0])
                continue
            parts[turn][core] = part(turn, core)
            block = parts[turn][core]
            if len(sent) >= 2:
                block = after(block, sent[-2])
            if turn == 2 and core == 1:
                half = block.shape[1] // 2
                first = send(block[:, :half], inwards)
                second = send(block[:, half:], inwards)
                got[turn][core] = (first, second)
                swapped[turn][core] = send(add(parts[turn - 1][core], got[turn - 1][core]), across)
                continue
            got[turn][core] = send(block, inwards)
            sent.append(got[turn][core])
            if turn:
                swapped[turn][core] = send(add(parts[turn - 1][core], got[turn - 1][core]), across)
    out = []
    for core in range(2):
        last = part(3, core)
        back = send(add(parts[2][core], swapped[1][core]), outwards)
        if core:
            rest = [last, swapped[2][core], back]
            half = last.shape[1] // 2
            out += [add(*[a[:, i * half : (i + 1) * half] for a in rest], got[2][core][i]) for i in range(2)]
        else:
            out.append(add(last, got[2][core], swapped[2][core], back))
    return (jnp.concatenate(gated, axis=1), jnp.concatenate(out, axis=1))


def solution(mesh):
    placed = (
        P("seq", None),
        P("seq", None, "chan"),
        P(None, "chan"),
        P(None, "chan"),
        P("chan"),
        P("seq", "chan"),
    )
    return jax.shard_map(
        local,
        mesh=mesh,
        in_specs=placed,
        out_specs=(P("seq", "chan"), P("seq", "chan")),
        check_vma=False,
    )
```

```python
import functools

import jax
import jax.numpy as jnp
from jax import lax
from jax.experimental import pallas as pl
from jax.experimental.pallas import tpu as pltpu
from jax.sharding import PartitionSpec as P

LANES = 128
WIDTHS = (256, 256)
SUBS = 8
MODES = 16
BLOCKS = 8
VMEM_BYTES = 60 * 1024 * 1024


def coefficients(residues, decay_rates, rows):
    return jnp.stack(
        [
            jnp.exp(-decay_rates),
            residues * jnp.sqrt(-jnp.expm1(-2.0 * decay_rates)),
            jnp.exp(-decay_rates * (rows // SUBS)),
            jnp.exp(-decay_rates * rows),
        ]
    )


def spread(coef_ref, which, lanes):
    table = coef_ref[which, :, lanes]
    return [jnp.broadcast_to(table[r : r + 1, :], (SUBS, LANES)) for r in range(MODES)]


def end_states(signal_ref, lanes, decay, run, backward):
    def step(j, state):
        at = run - 1 - j if backward else j
        row = signal_ref[pl.ds(at, SUBS, stride=run), lanes]
        return tuple(a * s + row for a, s in zip(decay, state))

    zero = jnp.zeros((SUBS, LANES), jnp.float32)
    return lax.fori_loop(0, run, step, (zero,) * MODES, unroll=8)


def full_scan(signal_ref, out_ref, decay, gain, state, run, backward):
    def step(j, state):
        at = run - 1 - j if backward else j
        rows = pl.ds(at, SUBS, stride=run)
        row = signal_ref[rows, :]
        state = tuple(a * s + row for a, s in zip(decay, state))
        terms = [g * s for g, s in zip(gain, state)]
        while len(terms) > 1:
            terms = [terms[i] + terms[i + 1] for i in range(0, len(terms), 2)]
        out_ref[rows, :] = terms[0]
        return state

    lax.fori_loop(0, run, step, tuple(state), unroll=8)


def bring(sources, targets, sems):
    copies = [pltpu.make_async_copy(a, b, sems.at[i]) for i, (a, b) in enumerate(zip(sources, targets))]
    for copy in copies:
        copy.start()
    return copies


def product(order_ref, x_ref, pieces, halves, x, w, x_sems, w_sems):
    depth = x.shape[2]
    width = w.shape[2] // 3
    loads, at = [], 0
    for r, parts in enumerate(halves):
        columns = pl.ds(pl.multiple_of(order_ref[r] * depth, depth), depth)
        load = bring([x_ref.at[:, columns]], [x.at[r]], x_sems.at[pl.ds(r, 1)])
        part = depth // parts
        for i in range(parts):
            targets = [w.at[r, pl.ds(i * part, part), pl.ds(b * width, width)] for b in range(3)]
            load += bring([pieces[at].at[b] for b in range(3)], targets, w_sems.at[at])
            at += 1
        loads.append(load)
    total = None
    for r in range(len(halves)):
        for copy in loads[r]:
            copy.wait()
        term = jnp.dot(x[r], w[r], preferred_element_type=jnp.float32)
        total = term if total is None else total + term
    return total


def project_part_kernel(halves, order_ref, x_ref, *refs):
    count = sum(halves)
    pieces, (out_ref, x, w, x_sems, w_sems) = refs[:count], refs[count:]
    out_ref[...] = product(order_ref, x_ref, pieces, halves, x, w, x_sems, w_sems)


def project_kernel(run, halves, order_ref, x_ref, *refs):
    count = sum(halves)
    pieces, refs = refs[:count], refs[count:]
    part_ref, g_ref, coef_ref, proj_ref, runs_ref, ends_ref, x, w, mix, gmix, x_sems, w_sems = refs
    width = g_ref.shape[1]
    total = part_ref[...] + product(order_ref, x_ref, pieces, halves, x, w, x_sems, w_sems)
    for b in range(3):
        proj_ref[b] = total[:, b * width : (b + 1) * width].astype(jnp.bfloat16)
    for lane in range(0, width, LANES):
        lanes = slice(lane, lane + LANES)
        mix[...] = proj_ref[1, :, lanes].astype(jnp.float32) * proj_ref[2, :, lanes].astype(jnp.float32)
        gmix[...] = g_ref[:, lanes].astype(jnp.float32) * proj_ref[0, :, lanes].astype(jnp.float32)
        decay = spread(coef_ref, 0, lanes)
        long = coef_ref[2, :, lanes]
        for way, signal in enumerate((mix, gmix)):
            state = end_states(signal, slice(None), decay, run, way == 1)
            for r in range(MODES):
                runs_ref[way, lane // LANES, pl.ds(r, SUBS, stride=MODES), :] = state[r]
            total = jnp.zeros((MODES, LANES), jnp.float32)
            for i in range(SUBS):
                at = SUBS - 1 - i if way else i
                total = long * total + runs_ref[way, lane // LANES, at * MODES : (at + 1) * MODES, :]
            ends_ref[way, :, lanes] = total


def scan_kernel(run, place_ref, proj_ref, g_ref, coef_ref, skip_ref, runs_ref, ends_ref, gated_ref, gp_ref, mix, out, start):
    me = place_ref[0]
    count = ends_ref.shape[0]
    width = g_ref.shape[1]
    for lane in range(0, width, LANES):
        lanes = slice(lane, lane + LANES)
        decay = spread(coef_ref, 0, lanes)
        gain = spread(coef_ref, 1, lanes)
        long = coef_ref[2, :, lanes]
        whole = coef_ref[3, :, lanes]
        skip = skip_ref[:, lanes]
        grad = g_ref[:, lanes].astype(jnp.float32)
        query, key, value = [proj_ref[b, :, lanes].astype(jnp.float32) for b in range(3)]
        for way in range(2):
            state = jnp.zeros((MODES, LANES), jnp.float32)
            for i in range(count - 1):
                at = count - 1 - i if way else i
                keep = me < at if way else at < me
                state = jnp.where(keep, whole * state + ends_ref[at, way, :, lanes], state)
            for i in range(SUBS):
                at = SUBS - 1 - i if way else i
                start[at * MODES : (at + 1) * MODES, :] = state
                state = long * state + runs_ref[way, lane // LANES, at * MODES : (at + 1) * MODES, :]
            first = [start[pl.ds(r, SUBS, stride=MODES), :] for r in range(MODES)]
            mix[...] = grad * query if way else key * value
            full_scan(mix, out, decay, gain, first, run, way == 1)
            filtered = out[...] + skip * mix[...]
            if way:
                gp_ref[:, width + lane : width + lane + LANES] = (filtered * value).astype(jnp.bfloat16)
                gp_ref[:, 2 * width + lane : 2 * width + lane + LANES] = (filtered * key).astype(jnp.bfloat16)
            else:
                gated_ref[:, lanes] = (query * filtered).astype(jnp.bfloat16)
                gp_ref[:, lane : lane + LANES] = (grad * filtered).astype(jnp.bfloat16)


def at_rest(shape):
    return pl.BlockSpec(shape, lambda *_: (0,) * len(shape))


def away():
    return pl.BlockSpec(memory_space=pltpu.HBM)


def block_scratch(tokens, pieces, width):
    rows, inputs = tokens.shape
    depth = inputs // BLOCKS
    parts = [len(piece) for piece in pieces]
    buffers = [
        pltpu.VMEM((len(pieces), rows, depth), tokens.dtype),
        pltpu.VMEM((len(pieces), depth, 3 * width), tokens.dtype),
    ]
    return parts, buffers, [pltpu.SemaphoreType.DMA((len(pieces),)), pltpu.SemaphoreType.DMA((sum(parts), 3))]


def product_cost(tokens, pieces, width):
    rows = tokens.shape[0]
    depth = tokens.shape[1] // BLOCKS * len(pieces)
    return pl.CostEstimate(
        flops=2 * rows * depth * 3 * width, bytes_accessed=2 * depth * (rows + 3 * width), transcendentals=0
    )


def project_part(order, tokens, pieces):
    rows = tokens.shape[0]
    flat = [part for piece in pieces for part in piece]
    width = flat[0].shape[2]
    halves, buffers, sems = block_scratch(tokens, pieces, width)
    return pl.pallas_call(
        functools.partial(project_part_kernel, halves),
        grid_spec=pltpu.PrefetchScalarGridSpec(
            num_scalar_prefetch=1,
            grid=(1,),
            in_specs=[away()] * (1 + len(flat)),
            out_specs=at_rest((rows, 3 * width)),
            scratch_shapes=buffers + sems,
        ),
        out_shape=jax.ShapeDtypeStruct((rows, 3 * width), jnp.float32),
        compiler_params=pltpu.CompilerParams(vmem_limit_bytes=48 * 1024 * 1024),
        cost_estimate=product_cost(tokens, pieces, width),
        name="project_part",
    )(order, tokens, *flat)


def project(order, tokens, pieces, part, grad_out, coef):
    rows = tokens.shape[0]
    width = grad_out.shape[1]
    flat = [part for piece in pieces for part in piece]
    groups = width // LANES
    halves, buffers, sems = block_scratch(tokens, pieces, width)
    return pl.pallas_call(
        functools.partial(project_kernel, rows // SUBS, halves),
        grid_spec=pltpu.PrefetchScalarGridSpec(
            num_scalar_prefetch=1,
            grid=(1,),
            in_specs=[away()] * (1 + len(flat)) + [at_rest(a.shape) for a in (part, grad_out, coef)],
            out_specs=[
                at_rest((3, rows, width)),
                at_rest((2, groups, SUBS * MODES, LANES)),
                at_rest((2, MODES, width)),
            ],
            scratch_shapes=buffers
            + [
                pltpu.VMEM((rows, LANES), jnp.float32),
                pltpu.VMEM((rows, LANES), jnp.float32),
            ]
            + sems,
        ),
        out_shape=[
            jax.ShapeDtypeStruct((3, rows, width), jnp.bfloat16),
            jax.ShapeDtypeStruct((2, groups, SUBS * MODES, LANES), jnp.float32),
            jax.ShapeDtypeStruct((2, MODES, width), jnp.float32),
        ],
        compiler_params=pltpu.CompilerParams(vmem_limit_bytes=48 * 1024 * 1024),
        cost_estimate=product_cost(tokens, pieces, width),
        name="project",
    )(order, tokens, *flat, part, grad_out, coef)


def scan(place, proj, grad_out, coef, skip, runs, ends):
    _, rows, width = proj.shape
    return pl.pallas_call(
        functools.partial(scan_kernel, rows // SUBS),
        grid_spec=pltpu.PrefetchScalarGridSpec(
            num_scalar_prefetch=1,
            grid=(1,),
            in_specs=[at_rest(a.shape) for a in (proj, grad_out, coef, skip, runs, ends)],
            out_specs=[at_rest((rows, width)), at_rest((rows, 3 * width))],
            scratch_shapes=[
                pltpu.VMEM((rows, LANES), jnp.float32),
                pltpu.VMEM((rows, LANES), jnp.float32),
                pltpu.VMEM((SUBS * MODES, LANES), jnp.float32),
            ],
        ),
        out_shape=[
            jax.ShapeDtypeStruct((rows, width), jnp.bfloat16),
            jax.ShapeDtypeStruct((rows, 3 * width), jnp.bfloat16),
        ],
        compiler_params=pltpu.CompilerParams(vmem_limit_bytes=48 * 1024 * 1024),
        cost_estimate=pl.CostEstimate(flops=rows * width * MODES * 16, bytes_accessed=12 * rows * width, transcendentals=0),
        name="scan",
    )(place, proj, grad_out, coef, skip, runs, ends)


def input_grad_kernel(halves, half, pick_ref, *refs):
    chunks = len(halves)
    counts = [sum(h) for h in halves]
    places, total = [], 0
    for c in range(chunks):
        width = refs[c].shape[1] // 3
        places.append([slice(total + b * width, total + (b + 1) * width) for b in range(3)])
        total += 3 * width
    grads, refs = refs[:chunks], refs[chunks:]
    pieces, refs = refs[: sum(counts)], refs[sum(counts) :]
    out_ref, weights, sems = refs
    r_wanted = pick_ref[0]
    depth = weights.shape[0]
    at = 0
    for c, parts_of in enumerate(halves):
        for r, parts in enumerate(parts_of):

            @pl.when(r_wanted == r)
            def _(c=c, r=r, parts=parts, at=at):
                if half is None:
                    part = depth // parts
                    moves = [(pieces[at + i], slice(i * part, (i + 1) * part)) for i in range(parts)]
                elif parts == 2:
                    moves = [(pieces[at + half], slice(0, depth))]
                else:
                    moves = [(pieces[at].at[:, half * depth : (half + 1) * depth, :], slice(0, depth))]
                for source, rows in moves:
                    for b in range(3):
                        pltpu.make_async_copy(source.at[b], weights.at[rows, places[c][b]], sems.at[c, b]).start()

            at += parts
    left = jnp.concatenate([g[...] for g in grads], axis=1)
    for c in range(chunks):
        for b in range(3):
            place = weights.at[:, places[c][b]]
            pltpu.make_async_copy(place, place, sems.at[c, b]).wait()
    tile = depth // 2

    @pl.loop(0, depth // tile)
    def _(i):
        here = pl.ds(pl.multiple_of(i * tile, tile), tile)
        total = lax.dot_general(left, weights[here, :], (((1,), (1,)), ((), ())), preferred_element_type=jnp.float32)
        out_ref[:, here] = total.astype(jnp.bfloat16)


def input_grad(pick, grads, weights, half=None):
    rows = grads[0].shape[0]
    depth = weights[0][0][0].shape[1] // (1 if half is None else 2)
    inner = sum(g.shape[1] for g in grads)
    halves = [[len(piece) for piece in pieces] for pieces in weights]
    flat = [part for pieces in weights for piece in pieces for part in piece]
    return pl.pallas_call(
        functools.partial(input_grad_kernel, halves, half),
        grid_spec=pltpu.PrefetchScalarGridSpec(
            num_scalar_prefetch=1,
            grid=(1,),
            in_specs=[at_rest(g.shape) for g in grads] + [away()] * len(flat),
            out_specs=at_rest((rows, depth)),
            scratch_shapes=[
                pltpu.VMEM((depth, inner), jnp.bfloat16),
                pltpu.SemaphoreType.DMA((len(grads), 3)),
            ],
        ),
        out_shape=jax.ShapeDtypeStruct((rows, depth), jnp.bfloat16),
        compiler_params=pltpu.CompilerParams(vmem_limit_bytes=(60 if half is None else 32) * 1024 * 1024),
        cost_estimate=pl.CostEstimate(
            flops=2 * rows * depth * inner, bytes_accessed=2 * (inner * (rows + depth) + rows * depth), transcendentals=0
        ),
        name="input_grad",
    )(pick, *grads, *flat)


def exchange(array, axis, bit):
    count = lax.axis_size(axis)
    return lax.ppermute(array, axis, [(i, i ^ bit) for i in range(count)])


def after(value, *others):
    return lax.optimization_barrier((value, *others))[0]


class Plane:
    def __init__(self, blocks):
        self.blocks = blocks
        self.held = [{} for _ in blocks]

    def own(self, c, *gate):
        mine = after(self.blocks[c], *gate) if gate else self.blocks[c]
        self.held[c][2] = [(exchange(mine, "seq", 2),)]
        self.held[c][4] = [(exchange(mine, "seq", 4),)]
        self.held[c][0] = [(mine, exchange(mine, "seq", 1))]

    def came(self, c, *places):
        return [part[0] for where in places for part in self.held[c][where]]

    def swapped(self, c, *places):
        return [part[1] for where in places for part in self.held[c][where]]

    def relay(self, c, *gate):
        far_x, far_y = self.came(c, 2, 4)
        axis = far_x.ndim - 2
        half = far_x.shape[axis] // 2
        low = lax.slice_in_dim(far_x, 0, half, axis=axis)
        high = lax.slice_in_dim(far_y, half, 2 * half, axis=axis)
        if gate:
            low, high = after((low, high), *gate)
        self.held[c][6] = [(exchange(low, "seq", 4),), (exchange(high, "seq", 2),)]

    def swap(self, c, places, *gate):
        for where in places:
            blocks = self.came(c, where)
            if gate:
                blocks = after(blocks, *gate)
            self.held[c][where] = [(part[0], exchange(block, "seq", 1)) for part, block in zip(self.held[c][where], blocks)]

    def pieces(self, c, places=(0, 2, 4, 6)):
        return [[pair[core] for pair in self.held[c][where]] for where in places for core in (0, 1)]


def gather_whole(mine):
    whole = lax.all_gather(mine, "seq", axis=1, tiled=True)
    return [[piece] for piece in jnp.split(whole, BLOCKS, axis=1)]


def local(tokens, proj_weight, residues, decay_rates, skip_gain, grad_out):
    rows = tokens.shape[0]
    depth = proj_weight.shape[0]
    channels = skip_gain.shape[0]
    groups = lax.axis_size("chan")
    me = lax.axis_index("seq").astype(jnp.int32)
    z = lax.axis_index("chan").astype(jnp.int32)
    direct = lax.axis_size("seq") == BLOCKS and groups == 4
    order = jnp.arange(BLOCKS, dtype=jnp.int32)
    if direct:
        order = order ^ me
    coef = coefficients(residues, decay_rates, rows)
    skip = skip_gain[None, :]
    branches = proj_weight.swapaxes(0, 1)
    slots, first = [], 0
    while first < channels:
        width = WIDTHS[min(len(slots), len(WIDTHS) - 1)]
        slots.append(slice(first, first + width))
        first += width
    chunks = len(slots)
    mine = [branches[:, :, lanes] for lanes in slots]

    def forward(c, pieces, part):
        lanes = slots[c]
        count = len(pieces)
        return project(order[BLOCKS - count :], tokens, pieces, part, grad_out[:, lanes], coef[:, :, lanes])

    def meet(made):
        return lax.all_gather(jnp.concatenate([m[2] for m in made], axis=2), "seq")

    def scans(span, made, seen):
        gated, grads = [], []
        start = slots[span[0]].start
        for i, c in enumerate(span):
            lanes = slots[c]
            proj, runs, _ = made[i]
            ends = seen[:, :, :, lanes.start - start : lanes.stop - start]
            gate, grad = scan(me.reshape(1), proj, grad_out[:, lanes], coef[:, :, lanes], skip[:, lanes], runs, ends)
            gated.append(gate)
            grads.append(grad)
        return gated, grads

    if not direct:
        weights = [gather_whole(a) for a in mine]
        made = []
        for c in range(chunks):
            part = project_part(order[:6], tokens, weights[c][:6])
            made.append(forward(c, weights[c][6:], part))
        gated, grads = scans(range(chunks), made, meet(made))
        flat = [jnp.concatenate([p[0][b] for p in pieces], axis=0) for pieces in weights for b in range(3)]
        contract = (((1,), (1,)), ((), ()))
        dx = lax.dot_general(jnp.concatenate(grads, axis=1), jnp.concatenate(flat, axis=1), contract, preferred_element_type=jnp.float32)
        grad_tokens = lax.psum_scatter(dx.astype(jnp.bfloat16), "chan", scatter_dimension=1, tiled=True)
        return (jnp.concatenate(gated, axis=1), grad_tokens)

    plane = Plane(mine)
    near, far = (0, 2, 4), (6,)
    plane.own(0)
    plane.relay(0)
    plane.swap(0, (2, 4))
    plane.own(1, *plane.swapped(0, 0, 2, 4))
    plane.swap(0, far)
    part = project_part(order[:6], tokens, plane.pieces(0, near))
    made = [forward(0, plane.pieces(0, far), part)]
    seen = meet(made)
    plane.relay(1, seen)
    plane.swap(1, (2, 4), seen)
    gated, grads = scans((0,), made, seen)
    part = project_part(order[:6], tokens, plane.pieces(1, near))
    plane.swap(1, far, part, grads[0])
    made.append(forward(1, plane.pieces(1, far), part))
    late = scans((1,), made[1:], meet(made[1:]))
    gated, grads = gated + late[0], grads + late[1]
    weights = [plane.pieces(c) for c in range(chunks)]

    turns = jnp.array([[3, 2, 1, 0], [3, 2, 0, 1], [0, 1, 3, 2], [0, 1, 2, 3]], jnp.int32)[z]
    inwards, across, outwards = [(0, 1), (3, 2)], [(1, 2), (2, 1)], [(1, 0), (2, 3)]

    def part(turn, core, half=None):
        pick = me ^ (2 * turns[turn] + core)
        return input_grad(pick.reshape(1), grads, weights, half)

    def add(*terms):
        return sum(t.astype(jnp.float32) for t in terms).astype(jnp.bfloat16)

    sent = []

    def send(block, pairs):
        return lax.ppermute(block, "chan", pairs)

    parts = [[None, None] for _ in range(4)]
    got = [[None, None] for _ in range(3)]
    swapped = [[None, None] for _ in range(3)]
    for turn in range(3):
        for core in range(2):
            if turn == core == 0:
                pair = [part(0, 0, half) for half in range(2)]
                parts[0][0] = jnp.concatenate(pair, axis=1)
                got[0][0] = jnp.concatenate([send(block, inwards) for block in pair], axis=1)
                sent.append(got[0][0])
                continue
            parts[turn][core] = part(turn, core)
            block = parts[turn][core]
            if len(sent) >= 2:
                block = after(block, sent[-2])
            if turn == 2 and core == 1:
                half = block.shape[1] // 2
                first = send(block[:, :half], inwards)
                second = send(block[:, half:], inwards)
                got[turn][core] = (first, second)
                swapped[turn][core] = send(add(parts[turn - 1][core], got[turn - 1][core]), across)
                continue
            got[turn][core] = send(block, inwards)
            sent.append(got[turn][core])
            if turn:
                swapped[turn][core] = send(add(parts[turn - 1][core], got[turn - 1][core]), across)
    out = []
    for core in range(2):
        last = part(3, core)
        back = send(add(parts[2][core], swapped[1][core]), outwards)
        if core:
            rest = add(last, swapped[2][core], back)
            half = last.shape[1] // 2
            out.append(add(rest[:, :half], got[2][core][0]))
            rest = rest[:, half:]
        else:
            out.append(add(last, got[2][core], swapped[2][core], back))
    base = jnp.pad(jnp.concatenate(out, axis=1), ((0, 0), (0, half)))
    base, rest = lax.optimization_barrier((base, rest))
    end = add(rest, got[2][1][1])
    return (jnp.concatenate(gated, axis=1), lax.dynamic_update_slice(base, end, (0, 3 * half)))


def solution(mesh):
    placed = (
        P("seq", None),
        P("seq", None, "chan"),
        P(None, "chan"),
        P(None, "chan"),
        P("chan"),
        P("seq", "chan"),
    )
    return jax.shard_map(
        local,
        mesh=mesh,
        in_specs=placed,
        out_specs=(P("seq", "chan"), P("seq", "chan")),
        check_vma=False,
    )
```
